32 devices in a mesh: groups: 1, wide: 32 (over z, y, x, core).
Axes of the slice: x: 2, y: 2, z: 4, core: 2. Of those that a mesh axis runs over, the one named last changes fastest.
Arguments:
- tokens: bfloat16 [128, 16384], P(('groups', 'wide')), may hold values from -6 to 6
- norm_gain: float32 [16384], replicated, may hold values from 0.1 to 1.9
- w_query: bfloat16 [16384, 16384], P(None, 'wide'), may hold values from -0.046875 to 0.046875
- w_keyval: bfloat16 [2048, 16384], P('wide'), may hold values from -0.046875 to 0.046875
- w_out: bfloat16 [16384, 16384], P(None, 'wide'), may hold values from -0.046875 to 0.046875
- cache_keys: bfloat16 [128, 8, 128, 128], P(('groups', 'wide'))
- cache_values: bfloat16 [128, 8, 128, 128], P(('groups', 'wide')), may hold values from -6 to 6
- session_ids: int32 [128], P('groups'), may hold values from 0 to 127, each once
- lengths: int32 [128], P(('groups', 'wide')), may hold values from 1 to 128, as said below
Outputs:
- attn_out: bfloat16 [128, 16384], P('groups', 'wide')
The draws below stay inside these ranges and needn't reach their ends.
Inputs may be any that keep to these rules, and one draw needn't show every extreme that they name: `session_ids`: a permutation of the sessions 0 to 127. `lengths`: some session has exactly 128 cached positions in every draw.
All inputs are finite; a program needn't handle non-finite values.
Results may differ from the reference program's by a relative error of at most 0.007.
The reference program's roundings to bfloat16 on the way count: a program that leaves them out, or rounds other values in their place, can miss the bound.
Values may be sent and summed in bfloat16 or wider, within the bound.
No kernel may reach another device: no remote copies, remote signals or barrier semaphores. Data moves between devices by JAX's collectives and lax.ppermute only.
A program may use at most 128 MiB of HBM per device.

```python
import math
import jax
import jax.numpy as jnp
from jax import lax

D = 16384
HEADS = 128
KVH = 8
HD = 128
CACHE_LEN = 128
SESSIONS = 128


def draw_cache_keys(key, part):
    key = jax.random.fold_in(key, 11)
    shape = (SESSIONS, KVH, CACHE_LEN, HD)
    return jax.random.normal(key, shape, jnp.float32).astype(jnp.bfloat16)


def draw_lengths(key, part):
    key = jax.random.fold_in(key, 23)
    drawn = jax.random.randint(key, (SESSIONS,), 1, CACHE_LEN + 1)
    picked = jax.random.randint(jax.random.fold_in(key, 1), (), 0, SESSIONS)
    return jnp.where(jnp.arange(SESSIONS) == picked, CACHE_LEN, drawn).astype(jnp.int32)


def level_of(stream_key, extent, pieces, low, largest):
    level = 1.0
    for axis_at, parts in pieces:
        steps = jax.random.uniform(jax.random.fold_in(jax.random.fold_in(stream_key, 6), axis_at), (parts,), jnp.float32, low / len(pieces), largest / len(pieces))
        level = level * jnp.repeat(jnp.exp(steps), extent[axis_at] // parts).reshape((-1,) + (1,) * (len(extent) - 1 - axis_at))
    return level


def gaussian(key, shape, scale, limit, split=(), held_as=jnp.bfloat16):
    result = scale * jax.random.normal(key, shape, jnp.float32)
    if split:
        result = result * level_of(key, shape, split, -0.22, 0.18)
    return jnp.clip(result, -limit, limit).astype(held_as)


def setup_inputs(seed: int = 0, part: int = 0) -> dict:
    seeds = jax.random.split(jax.random.key(seed), 10)
    own_keys = jax.random.split(jax.random.fold_in(seeds[9], part), 10)
    tokens = gaussian(own_keys[0], (SESSIONS, D), 1.0, 6.0, ((0, 32),))
    norm_gain = jnp.clip(1.0 + 0.18 * jax.random.normal(seeds[1], (D,), jnp.float32), 0.1, 1.9)
    w_query = gaussian(seeds[2], (D, D), D ** -0.5, 0.046875, ((1, 32),))
    w_keyval = gaussian(seeds[3], (2 * KVH * HD, D), D ** -0.5, 0.046875, ((0, 32),))
    w_out = gaussian(seeds[4], (D, D), D ** -0.5, 0.046875, ((1, 32),))
    cache_keys = draw_cache_keys(jax.random.fold_in(jax.random.fold_in(seeds[9], part), 71), part)
    cache_values = gaussian(own_keys[6], (SESSIONS, KVH, CACHE_LEN, HD), 1.0, 6.0, ((0, 32),))
    session_ids = jax.random.permutation(own_keys[7], SESSIONS).astype(jnp.int32)
    lengths = draw_lengths(jax.random.fold_in(jax.random.fold_in(seeds[9], part), 71), part)
    return dict(tokens=tokens, norm_gain=norm_gain, w_query=w_query, w_keyval=w_keyval, w_out=w_out, cache_keys=cache_keys, cache_values=cache_values, session_ids=session_ids, lengths=lengths)


ROPE_BASE = 500000.0

def rms_rows(rows, gain):
    values = rows.astype(jnp.float32)
    meansq = lax.optimization_barrier(jnp.mean(values * values, axis=-1, keepdims=True))
    return (values * lax.rsqrt(meansq + 1e-05) * gain).astype(jnp.bfloat16)

def rotate_heads(values, positions):
    width = values.shape[-1]
    halfway = width // 2
    indices = jnp.arange(halfway).astype(jnp.float32)
    inverse_freq = jnp.exp(indices * (-2.0 * math.log(ROPE_BASE) / width))
    angles = positions.astype(jnp.float32)[:, None, None] * inverse_freq
    cosine = jnp.cos(angles)
    sine = jnp.sin(angles)
    first = values[..., :halfway]
    second = values[..., halfway:]
    return jnp.concatenate([first * cosine - second * sine, second * cosine + first * sine], axis=-1)

def reference(tokens, norm_gain, w_query, w_keyval, w_out, cache_keys, cache_values, session_ids, lengths):
    normed = rms_rows(tokens, norm_gain)
    query = jnp.dot(normed, w_query, preferred_element_type=jnp.float32).astype(jnp.bfloat16)
    keyval = lax.dot_general(normed, w_keyval, (((1,), (1,)), ((), ())), preferred_element_type=jnp.float32).astype(jnp.bfloat16)
    inverse = jnp.argsort(session_ids).astype(jnp.int32)
    query_sess = query[inverse]
    keyval_sess = keyval[inverse]
    group = HEADS // KVH
    scale = HD ** (-0.5)
    rot_query = rotate_heads(query_sess.astype(jnp.float32).reshape(SESSIONS, HEADS, HD), lengths).astype(jnp.bfloat16)
    rot_query = rot_query.astype(jnp.float32).reshape(SESSIONS, KVH, group, HD)
    new_keys = keyval_sess[:, :KVH * HD].astype(jnp.float32).reshape(SESSIONS, KVH, HD)
    own_key = rotate_heads(new_keys, lengths).astype(jnp.bfloat16).astype(jnp.float32)
    own_value = keyval_sess[:, KVH * HD:].astype(jnp.float32).reshape(SESSIONS, KVH, HD)
    scores = jnp.einsum('sgqd,sgpd->sgqp', rot_query, cache_keys.astype(jnp.float32)) * scale
    valid = jnp.arange(CACHE_LEN)[None, :] < lengths[:, None]
    scores = jnp.where(valid[:, None, None, :], scores, -jnp.inf)
    own_score = jnp.einsum('sgqd,sgd->sgq', rot_query, own_key) * scale
    highest = jnp.maximum(lax.optimization_barrier(jnp.max(scores, axis=-1)), own_score)
    cached_exp = jnp.exp(scores - highest[..., None])
    own_exp = jnp.exp(own_score - highest)
    total = lax.optimization_barrier(jnp.sum(cached_exp, axis=-1)) + own_exp
    cached_weight = (cached_exp / total[..., None]).astype(jnp.bfloat16).astype(jnp.float32)
    own_weight = (own_exp / total).astype(jnp.bfloat16).astype(jnp.float32)
    attended = jnp.einsum('sgqp,sgpd->sgqd', cached_weight, cache_values.astype(jnp.float32))
    attended = attended + own_weight[..., None] * own_value[:, :, None, :]
    attended = attended.reshape(SESSIONS, D).astype(jnp.bfloat16)
    out_sess = jnp.dot(attended, w_out, preferred_element_type=jnp.float32)
    return out_sess[session_ids].astype(jnp.bfloat16)
```

```python
import functools
import math

import jax
import jax.numpy as jnp
from jax import lax
from jax.experimental import pallas as pl
from jax.experimental.pallas import tpu as pltpu
from jax.sharding import PartitionSpec as P

HEADS = 128
KVH = 8


ROPE_BASE = 500000.0

LANES = 128
PIECE = 4
TILE = 16
MIB = 1 << 20


def rms_rows(rows, gain):
    values = rows.astype(jnp.float32)
    meansq = jnp.mean(values * values, axis=-1, keepdims=True)
    return (values * lax.rsqrt(meansq + 1e-05) * gain).astype(jnp.bfloat16)


def rotate_heads(values, positions):
    width = values.shape[-1]
    halfway = width // 2
    indices = jnp.arange(halfway).astype(jnp.float32)
    inverse_freq = jnp.exp(indices * (-2.0 * math.log(ROPE_BASE) / width))
    angles = positions.astype(jnp.float32)[:, None, None] * inverse_freq
    cosine = jnp.cos(angles)
    sine = jnp.sin(angles)
    first = values[..., :halfway]
    second = values[..., halfway:]
    return jnp.concatenate(
        [first * cosine - second * sine, second * cosine + first * sine], axis=-1
    )


def attend_sessions(query_sess, keyval_sess, cache_keys, cache_values, lengths):
    sessions = query_sess.shape[0]
    head_dim = query_sess.shape[1] // HEADS
    group = HEADS // KVH
    scale = head_dim ** (-0.5)
    rot_query = rotate_heads(
        query_sess.astype(jnp.float32).reshape(sessions, HEADS, head_dim), lengths
    )
    rot_query = rot_query.astype(jnp.bfloat16).reshape(sessions, KVH, group, head_dim)
    new_keys = keyval_sess[:, : KVH * head_dim].astype(jnp.float32).reshape(sessions, KVH, head_dim)
    own_key = rotate_heads(new_keys, lengths).astype(jnp.bfloat16)
    own_value = keyval_sess[:, KVH * head_dim :].reshape(sessions, KVH, head_dim)
    scores = (
        jnp.einsum("sgqd,sgpd->sgqp", rot_query, cache_keys, preferred_element_type=jnp.float32)
        * scale
    )
    valid = jnp.arange(cache_keys.shape[2])[None, :] < lengths[:, None]
    scores = jnp.where(valid[:, None, None, :], scores, -jnp.inf)
    own_score = (
        jnp.einsum("sgqd,sgd->sgq", rot_query, own_key, preferred_element_type=jnp.float32) * scale
    )
    highest = jnp.maximum(jnp.max(scores, axis=-1), own_score)
    cached_exp = jnp.exp(scores - highest[..., None])
    own_exp = jnp.exp(own_score - highest)
    total = jnp.sum(cached_exp, axis=-1) + own_exp
    cached_weight = (cached_exp / total[..., None]).astype(jnp.bfloat16)
    own_weight = (own_exp / total).astype(jnp.bfloat16)
    attended = jnp.einsum(
        "sgqp,sgpd->sgqd", cached_weight, cache_values, preferred_element_type=jnp.float32
    )
    attended = (
        attended
        + own_weight.astype(jnp.float32)[..., None] * own_value.astype(jnp.float32)[:, :, None, :]
    )
    return attended.reshape(sessions, HEADS * head_dim).astype(jnp.bfloat16)


def on_any(
    tokens, norm_gain, w_query, w_keyval, w_out, cache_keys, cache_values, session_ids, lengths
):
    normed = rms_rows(tokens, norm_gain)
    query_cols = w_query.shape[1]
    everyone = lax.all_gather(normed, "wide", axis=0, tiled=True)
    query_part = jnp.dot(everyone, w_query, preferred_element_type=jnp.float32).astype(jnp.bfloat16)
    keyval_part = lax.dot_general(
        everyone, w_keyval, (((1,), (1,)), ((), ())), preferred_element_type=jnp.float32
    ).astype(jnp.bfloat16)
    joined = jnp.concatenate([query_part, keyval_part], axis=1)
    inverse = jnp.argsort(session_ids)
    ordered = joined[inverse]
    query_local = ordered[:, :query_cols]
    keyval_local = ordered[:, query_cols:]
    query_sess, keyval_sess = (
        lax.all_to_all(query_local, "wide", split_axis=0, concat_axis=1, tiled=True),
        lax.all_to_all(keyval_local, "wide", split_axis=0, concat_axis=1, tiled=True),
    )
    attended = attend_sessions(query_sess, keyval_sess, cache_keys, cache_values, lengths)
    all_attended = lax.all_gather(attended, "wide", axis=0, tiled=True)
    out_sess = jnp.dot(all_attended, w_out, preferred_element_type=jnp.float32)
    return out_sess[session_ids].astype(jnp.bfloat16)


def norm_pack_kernel(own, z1, z2, z3, gain, low, high, full):
    width = own.shape[1]
    blocks = width // LANES
    pieces = (own, z1, z2, z3)
    scales = []
    for piece in pieces:
        values = piece[...].astype(jnp.float32)
        meansq = jnp.sum(values * values, axis=-1, keepdims=True) * (1.0 / width)
        scales.append(lax.rsqrt(meansq + 1e-05))
    for block in range(blocks):
        lanes = slice(block * LANES, (block + 1) * LANES)
        factor = gain[:, lanes]
        rows = jnp.concatenate(
            [piece[:, lanes].astype(jnp.float32) * scale * factor for piece, scale in zip(pieces, scales)],
            axis=0,
        ).astype(jnp.bfloat16)
        full[block] = rows
        if block < blocks // 2:
            low[block] = rows
        else:
            high[block - blocks // 2] = rows


def pack_kernel(own, z1, z2, z3, low, high, full):
    blocks = own.shape[0] // PIECE
    pieces = (own, z1, z2, z3)
    for first in range(0, blocks, 4):
        tiles = [
            piece[first * PIECE : (first + 4) * PIECE, :].astype(jnp.float32) for piece in pieces
        ]
        for at in range(4):
            block = first + at
            rows = jnp.concatenate(
                [tile[at * PIECE : (at + 1) * PIECE, :] for tile in tiles], axis=0
            ).astype(jnp.bfloat16)
            full[block] = rows
            if block < blocks // 2:
                low[block] = rows
            else:
                high[block - blocks // 2] = rows


def packed_shapes(blocks):
    half = jax.ShapeDtypeStruct((blocks // 2, TILE, LANES), jnp.bfloat16)
    return (half, half, jax.ShapeDtypeStruct((blocks, TILE, LANES), jnp.bfloat16))


def norm_pack(own, z1, z2, z3, gain):
    blocks = own.shape[1] // LANES
    return pl.pallas_call(
        norm_pack_kernel,
        out_shape=packed_shapes(blocks),
        compiler_params=pltpu.CompilerParams(vmem_limit_bytes=24 * MIB),
        cost_estimate=pl.CostEstimate(flops=4_000_000, bytes_accessed=2_000_000, transcendentals=0),
    )(own, z1, z2, z3, gain[None, :])


def pack(own, z1, z2, z3):
    blocks = own.shape[0] // PIECE
    return pl.pallas_call(
        pack_kernel,
        out_shape=packed_shapes(blocks),
        compiler_params=pltpu.CompilerParams(vmem_limit_bytes=24 * MIB),
        cost_estimate=pl.CostEstimate(flops=1_000_000, bytes_accessed=2_000_000, transcendentals=0),
    )(own, z1, z2, z3)


def swapped(array, mask, devices):
    return lax.ppermute(array, "wide", [(i, i ^ mask) for i in range(devices)])


def gather_rows(piece, pack_pieces, devices):
    swap = functools.partial(swapped, devices=devices)
    z2, z3, z1 = swap(piece, 16), swap(piece, 24), swap(piece, 8)
    low, high, full = pack_pieces(piece, z1, z2, z3)
    x_low, y_high = swap(low, 2), swap(high, 4)
    x_high, y_low = swap(high, 2), swap(low, 4)
    d_low, d_high = swap(x_low, 4), swap(y_high, 2)
    other = swap(full, 1)
    mine = [(low, high), (x_low, x_high), (y_low, y_high), (d_low, d_high)]
    theirs = [(swap(a, 1), swap(b, 1)) for a, b in mine[1:]]
    return mine, other, theirs


def row_devices(devices):
    rows = jnp.arange(devices * PIECE, dtype=jnp.int32)
    core = rows // (devices * PIECE // 2)
    plane = (rows // TILE) % 4
    column = (rows // PIECE) % 4
    me = lax.axis_index("wide").astype(jnp.int32)
    return (me ^ (core + 2 * plane + 8 * column)) * PIECE + rows % PIECE


def gathered_tile(refs, count):
    blocks = []
    for block in range(count):
        blocks.append(jnp.concatenate([ref[block] for ref in refs], axis=0))
    return jnp.concatenate(blocks, axis=1)


def query_kernel(*refs, steps):
    low, high = refs[0:8], refs[8:16]
    weight, weight_kv, codes, sess, parity, out, total, total_kv = refs[16:]
    step = pl.program_id(0)
    count = low[0].shape[0]

    @pl.when(step == 0)
    def _():
        total[...] = jnp.zeros_like(total)
        total_kv[...] = jnp.zeros_like(total_kv)

    def add(parts):
        rows = gathered_tile(parts, count)
        total[...] += jnp.dot(rows, weight[...], preferred_element_type=jnp.float32)
        total_kv[...] += lax.dot_general(
            rows, weight_kv[...], (((1,), (1,)), ((), ())), preferred_element_type=jnp.float32
        )

    pl.when(step < steps // 2)(lambda: add(low))
    pl.when(step >= steps // 2)(lambda: add(high))

    @pl.when(step == steps - 1)
    def _():
        rows, width = total.shape
        heads = width // LANES
        stacked = jnp.concatenate(
            [total[:, h * LANES : (h + 1) * LANES].astype(jnp.bfloat16) for h in range(heads)], axis=0
        )
        at = lax.broadcasted_iota(jnp.int32, (rows * heads, rows * heads), 0)
        wanted = ((at // PIECE) % heads) * rows + (at // (PIECE * heads)) * PIECE + at % PIECE
        chosen = (wanted == codes[...]).astype(jnp.float32).astype(jnp.bfloat16)
        query = jnp.dot(chosen, stacked, preferred_element_type=jnp.float32).astype(jnp.bfloat16)
        devices = rows // PIECE
        out[:, 0:TILE, :] = query.reshape(devices, TILE, LANES)
        columns = total_kv.shape[1]
        keyval = total_kv[...].astype(jnp.bfloat16)
        at = lax.broadcasted_iota(jnp.int32, (devices * TILE, rows), 0)
        wanted = jnp.where(at % TILE < PIECE, (at // TILE) * PIECE + at % TILE, -1)
        chosen = (wanted == sess[...]).astype(jnp.float32).astype(jnp.bfloat16)
        ordered = jnp.dot(chosen, keyval, preferred_element_type=jnp.float32).astype(jnp.bfloat16)
        here = lax.broadcasted_iota(jnp.int32, (columns, LANES), 0)
        there = lax.broadcasted_iota(jnp.int32, (columns, LANES), 1)
        place = (there == here + parity[0] * columns).astype(jnp.float32).astype(jnp.bfloat16)
        placed = jnp.dot(ordered, place, preferred_element_type=jnp.float32).astype(jnp.bfloat16)
        out[:, TILE : 2 * TILE, :] = placed.reshape(devices, TILE, LANES)


def out_kernel(*refs, steps):
    low, high = refs[0:8], refs[8:16]
    weight, sess, wanted, out, total = refs[16:]
    step = pl.program_id(0)
    count = low[0].shape[0]

    @pl.when(step == 0)
    def _():
        total[...] = jnp.zeros_like(total)

    def add(parts):
        rows = gathered_tile(parts, count)
        total[...] += jnp.dot(rows, weight[...], preferred_element_type=jnp.float32)

    pl.when(step < steps // 2)(lambda: add(low))
    pl.when(step >= steps // 2)(lambda: add(high))

    @pl.when(step == steps - 1)
    def _():
        chosen = (wanted[...] == sess[...]).astype(jnp.float32).astype(jnp.bfloat16)
        rounded = total[...].astype(jnp.bfloat16)
        out[...] = jnp.dot(chosen, rounded, preferred_element_type=jnp.float32).astype(jnp.bfloat16)


STEPS = 16


def gathered_operands(gathered, steps):
    mine, other, theirs = gathered
    blocks = other.shape[0]
    count = blocks // steps
    operands, specs = [], []
    for half in range(2):
        if half == 0:
            index = lambda k: (jnp.minimum(k, steps // 2 - 1), 0, 0)
            index_full = index
        else:
            index = lambda k: (jnp.maximum(k - steps // 2, 0), 0, 0)
            index_full = lambda k: (jnp.maximum(k, steps // 2), 0, 0)
        block = (count, TILE, LANES)
        for pair in mine:
            operands.append(pair[half])
            specs.append(pl.BlockSpec(block, index))
        operands.append(other)
        specs.append(pl.BlockSpec(block, index_full))
        for pair in theirs:
            operands.append(pair[half])
            specs.append(pl.BlockSpec(block, index))
    return operands, specs


def project_query(gathered, w_query, w_keyval, sess, devices):
    operands, specs = gathered_operands(gathered, STEPS)
    depth, columns = w_query.shape
    rows = devices * PIECE
    heads = columns // LANES
    codes = (jnp.arange(heads, dtype=jnp.int32)[:, None] * rows + sess[None, :]).reshape(1, -1)
    parity = (lax.axis_index("wide") % 2).astype(jnp.int32)[None]
    chunk = depth // STEPS
    return pl.pallas_call(
        functools.partial(query_kernel, steps=STEPS),
        grid=(STEPS,),
        in_specs=specs
        + [
            pl.BlockSpec((chunk, columns), lambda k: (k, 0)),
            pl.BlockSpec((w_keyval.shape[0], chunk), lambda k: (0, k)),
            pl.BlockSpec((1, heads * rows), lambda k: (0, 0)),
            pl.BlockSpec((1, rows), lambda k: (0, 0)),
            pl.BlockSpec(memory_space=pltpu.SMEM),
        ],
        out_specs=pl.BlockSpec((devices, 2 * TILE, LANES), lambda k: (0, 0, 0)),
        out_shape=jax.ShapeDtypeStruct((devices, 2 * TILE, LANES), jnp.bfloat16),
        scratch_shapes=[
            pltpu.VMEM((rows, columns), jnp.float32),
            pltpu.VMEM((rows, w_keyval.shape[0]), jnp.float32),
        ],
        compiler_params=pltpu.CompilerParams(vmem_limit_bytes=24 * MIB),
        cost_estimate=pl.CostEstimate(
            flops=2 * rows * depth * columns, bytes_accessed=2 * depth * (columns + rows), transcendentals=0
        ),
    )(*operands, w_query, w_keyval, codes, sess[None, :], parity)


def project_out(gathered, w_out, sess, wanted, devices):
    operands, specs = gathered_operands(gathered, STEPS)
    depth, columns = w_out.shape
    rows = devices * PIECE
    chunk = depth // STEPS
    return pl.pallas_call(
        functools.partial(out_kernel, steps=STEPS),
        grid=(STEPS,),
        in_specs=specs
        + [
            pl.BlockSpec((chunk, columns), lambda k: (k, 0)),
            pl.BlockSpec((1, rows), lambda k: (0, 0)),
            pl.BlockSpec((rows, 1), lambda k: (0, 0)),
        ],
        out_specs=pl.BlockSpec((rows, columns), lambda k: (0, 0)),
        out_shape=jax.ShapeDtypeStruct((rows, columns), jnp.bfloat16),
        scratch_shapes=[pltpu.VMEM((rows, columns), jnp.float32)],
        compiler_params=pltpu.CompilerParams(vmem_limit_bytes=24 * MIB),
        cost_estimate=pl.CostEstimate(
            flops=2 * rows * depth * columns, bytes_accessed=2 * depth * (columns + rows), transcendentals=0
        ),
    )(*operands, w_out, sess[None, :], wanted[:, None])


def attend_kernel(received, keys, values, cosine, sine, limits, out):
    sessions, kv_heads, cache_len, width = keys.shape
    devices = received.shape[0]
    per_group = devices // kv_heads
    rows = per_group * TILE
    scale = width ** (-0.5)

    def rotate(vectors):
        count = vectors.shape[0]
        return (
            vectors * cosine[0:count, :] + pltpu.roll(vectors, width // 2, 1) * sine[0:count, :]
        ).astype(jnp.bfloat16)

    own = received[:, TILE : 2 * TILE, :].astype(jnp.float32)
    pairs = devices // 2
    own = own.reshape(pairs, 2, TILE, width)
    own = own[:, 0] + own[:, 1]
    own = own[:, 0:8]
    own_rows = kv_heads * 8
    own_key = rotate(own[0:kv_heads].reshape(own_rows, width))
    own_value = own[kv_heads:].reshape(own_rows, width).astype(jnp.bfloat16)

    session = lax.broadcasted_iota(jnp.int32, (rows, sessions * cache_len), 0) % PIECE
    column = lax.broadcasted_iota(jnp.int32, (rows, sessions * cache_len), 1)
    valid = (column // cache_len == session) & (column % cache_len < limits[...])
    own_session = lax.broadcasted_iota(jnp.int32, (rows, own_rows), 0) % PIECE
    own_column = lax.broadcasted_iota(jnp.int32, (rows, own_rows), 1)
    for group in range(kv_heads):
        query = received[group * per_group : (group + 1) * per_group, 0:TILE, :]
        query = rotate(query.reshape(rows, width).astype(jnp.float32))
        group_keys = keys[:, group].reshape(sessions * cache_len, width)
        group_values = values[:, group].reshape(sessions * cache_len, width)
        contract = (((1,), (1,)), ((), ()))
        scores = (
            lax.dot_general(query, group_keys, contract, preferred_element_type=jnp.float32) * scale
        )
        scores = jnp.where(valid, scores, -jnp.inf)
        own_scores = (
            lax.dot_general(query, own_key, contract, preferred_element_type=jnp.float32) * scale
        )
        own_scores = jnp.where(own_column == group * 8 + own_session, own_scores, -jnp.inf)
        highest = jnp.maximum(
            jnp.max(scores, axis=-1, keepdims=True), jnp.max(own_scores, axis=-1, keepdims=True)
        )
        cached_exp = jnp.exp(scores - highest)
        own_exp = jnp.exp(own_scores - highest)
        total = jnp.sum(cached_exp, axis=-1, keepdims=True) + jnp.sum(
            own_exp, axis=-1, keepdims=True
        )
        weights = (cached_exp / total).astype(jnp.bfloat16)
        own_weights = (own_exp / total).astype(jnp.bfloat16)
        attended = jnp.dot(weights, group_values, preferred_element_type=jnp.float32)
        attended += jnp.dot(own_weights, own_value, preferred_element_type=jnp.float32)
        out[group * rows : (group + 1) * rows, :] = attended.astype(jnp.bfloat16)


def attend(received, keys, values, lengths):
    sessions, kv_heads, cache_len, width = keys.shape
    devices = received.shape[0]
    rows = devices // kv_heads * TILE
    halfway = width // 2
    indices = jnp.arange(halfway).astype(jnp.float32)
    inverse_freq = jnp.exp(indices * (-2.0 * math.log(ROPE_BASE) / width))
    angles = lengths.astype(jnp.float32)[:, None] * inverse_freq
    cosine = jnp.cos(angles)
    sine = jnp.sin(angles)
    cosine = jnp.tile(jnp.concatenate([cosine, cosine], axis=1), (rows // sessions, 1))
    sine = jnp.tile(jnp.concatenate([-sine, sine], axis=1), (rows // sessions, 1))
    limits = jnp.repeat(lengths, cache_len)[None, :]
    return pl.pallas_call(
        attend_kernel,
        out_shape=jax.ShapeDtypeStruct((devices * TILE, width), jnp.bfloat16),
        compiler_params=pltpu.CompilerParams(vmem_limit_bytes=24 * MIB),
        cost_estimate=pl.CostEstimate(
            flops=150_000_000, bytes_accessed=3_000_000, transcendentals=300_000
        ),
    )(received, keys, values, cosine, sine, limits)


def on_block(
    tokens, norm_gain, w_query, w_keyval, w_out, cache_keys, cache_values, session_ids, lengths, devices
):
    source = row_devices(devices)
    pack_tokens = functools.partial(norm_pack, gain=norm_gain)
    gathered = gather_rows(tokens, pack_tokens, devices)
    local = project_query(gathered, w_query, w_keyval, session_ids[source], devices)
    received = lax.all_to_all(local, "wide", split_axis=0, concat_axis=0, tiled=True)
    attended = attend(received, cache_keys, cache_values, lengths)
    gathered = gather_rows(attended, pack, devices)
    return project_out(gathered, w_out, source, session_ids, devices)


def fits_block(devices, tokens, w_query, w_keyval, cache_keys):
    sessions, kv_heads, cache_len, width = cache_keys.shape
    return (
        devices == 32
        and tokens.shape[0] == PIECE
        and sessions == PIECE
        and width == LANES
        and cache_len == LANES
        and kv_heads == KVH
        and w_query.shape[1] == 4 * LANES
        and w_keyval.shape[0] == LANES // 2
    )


def on_device(*args, devices):
    tokens, _, w_query, w_keyval, _, cache_keys = args[:6]
    if fits_block(devices, tokens, w_query, w_keyval, cache_keys):
        return on_block(*args, devices)
    return on_any(*args)


def solution(mesh):
    return jax.shard_map(
        functools.partial(on_device, devices=mesh.shape["wide"]),
        mesh=mesh,
        in_specs=(
            P(("groups", "wide"), None),
            P(),
            P(None, "wide"),
            P("wide", None),
            P(None, "wide"),
            P(("groups", "wide"), None, None, None),
            P(("groups", "wide"), None, None, None),
            P("groups"),
            P(("groups", "wide")),
        ),
        out_specs=P("groups", "wide"),
        check_vma=False,
    )
```

```python
import functools
import math

import jax
import jax.numpy as jnp
from jax import lax
from jax.experimental import pallas as pl
from jax.experimental.pallas import tpu as pltpu
from jax.sharding import PartitionSpec as P

HEADS = 128
KVH = 8


ROPE_BASE = 500000.0

LANES = 128
PIECE = 4
TILE = 16
MIB = 1 << 20


def rms_rows(rows, gain):
    values = rows.astype(jnp.float32)
    meansq = jnp.mean(values * values, axis=-1, keepdims=True)
    return (values * lax.rsqrt(meansq + 1e-05) * gain).astype(jnp.bfloat16)


def rotate_heads(values, positions):
    width = values.shape[-1]
    halfway = width // 2
    indices = jnp.arange(halfway).astype(jnp.float32)
    inverse_freq = jnp.exp(indices * (-2.0 * math.log(ROPE_BASE) / width))
    angles = positions.astype(jnp.float32)[:, None, None] * inverse_freq
    cosine = jnp.cos(angles)
    sine = jnp.sin(angles)
    first = values[..., :halfway]
    second = values[..., halfway:]
    return jnp.concatenate(
        [first * cosine - second * sine, second * cosine + first * sine], axis=-1
    )


def attend_sessions(query_sess, keyval_sess, cache_keys, cache_values, lengths):
    sessions = query_sess.shape[0]
    head_dim = query_sess.shape[1] // HEADS
    group = HEADS // KVH
    scale = head_dim ** (-0.5)
    rot_query = rotate_heads(
        query_sess.astype(jnp.float32).reshape(sessions, HEADS, head_dim), lengths
    )
    rot_query = rot_query.astype(jnp.bfloat16).reshape(sessions, KVH, group, head_dim)
    new_keys = keyval_sess[:, : KVH * head_dim].astype(jnp.float32).reshape(sessions, KVH, head_dim)
    own_key = rotate_heads(new_keys, lengths).astype(jnp.bfloat16)
    own_value = keyval_sess[:, KVH * head_dim :].reshape(sessions, KVH, head_dim)
    scores = (
        jnp.einsum("sgqd,sgpd->sgqp", rot_query, cache_keys, preferred_element_type=jnp.float32)
        * scale
    )
    valid = jnp.arange(cache_keys.shape[2])[None, :] < lengths[:, None]
    scores = jnp.where(valid[:, None, None, :], scores, -jnp.inf)
    own_score = (
        jnp.einsum("sgqd,sgd->sgq", rot_query, own_key, preferred_element_type=jnp.float32) * scale
    )
    highest = jnp.maximum(jnp.max(scores, axis=-1), own_score)
    cached_exp = jnp.exp(scores - highest[..., None])
    own_exp = jnp.exp(own_score - highest)
    total = jnp.sum(cached_exp, axis=-1) + own_exp
    cached_weight = (cached_exp / total[..., None]).astype(jnp.bfloat16)
    own_weight = (own_exp / total).astype(jnp.bfloat16)
    attended = jnp.einsum(
        "sgqp,sgpd->sgqd", cached_weight, cache_values, preferred_element_type=jnp.float32
    )
    attended = (
        attended
        + own_weight.astype(jnp.float32)[..., None] * own_value.astype(jnp.float32)[:, :, None, :]
    )
    return attended.reshape(sessions, HEADS * head_dim).astype(jnp.bfloat16)


def on_any(
    tokens, norm_gain, w_query, w_keyval, w_out, cache_keys, cache_values, session_ids, lengths
):
    normed = rms_rows(tokens, norm_gain)
    query_cols = w_query.shape[1]
    everyone = lax.all_gather(normed, "wide", axis=0, tiled=True)
    query_part = jnp.dot(everyone, w_query, preferred_element_type=jnp.float32).astype(jnp.bfloat16)
    keyval_part = lax.dot_general(
        everyone, w_keyval, (((1,), (1,)), ((), ())), preferred_element_type=jnp.float32
    ).astype(jnp.bfloat16)
    joined = jnp.concatenate([query_part, keyval_part], axis=1)
    inverse = jnp.argsort(session_ids)
    ordered = joined[inverse]
    query_local = ordered[:, :query_cols]
    keyval_local = ordered[:, query_cols:]
    query_sess, keyval_sess = (
        lax.all_to_all(query_local, "wide", split_axis=0, concat_axis=1, tiled=True),
        lax.all_to_all(keyval_local, "wide", split_axis=0, concat_axis=1, tiled=True),
    )
    attended = attend_sessions(query_sess, keyval_sess, cache_keys, cache_values, lengths)
    all_attended = lax.all_gather(attended, "wide", axis=0, tiled=True)
    out_sess = jnp.dot(all_attended, w_out, preferred_element_type=jnp.float32)
    return out_sess[session_ids].astype(jnp.bfloat16)


def norm_pack_kernel(own, z1, z2, z3, gain, low, high, full):
    width = own.shape[1]
    blocks = width // LANES
    pieces = (own, z1, z2, z3)
    scales = []
    for piece in pieces:
        values = piece[...].astype(jnp.float32)
        meansq = jnp.sum(values * values, axis=-1, keepdims=True) * (1.0 / width)
        scales.append(lax.rsqrt(meansq + 1e-05))
    for block in range(blocks):
        lanes = slice(block * LANES, (block + 1) * LANES)
        factor = gain[:, lanes]
        rows = jnp.concatenate(
            [piece[:, lanes].astype(jnp.float32) * scale * factor for piece, scale in zip(pieces, scales)],
            axis=0,
        ).astype(jnp.bfloat16)
        full[block] = rows
        if block < blocks // 2:
            low[block] = rows
        else:
            high[block - blocks // 2] = rows


def pack_kernel(own, z1, z2, z3, low, high, full):
    blocks = own.shape[0] // PIECE
    pieces = (own, z1, z2, z3)
    for first in range(0, blocks, 4):
        tiles = [
            piece[first * PIECE : (first + 4) * PIECE, :].astype(jnp.float32) for piece in pieces
        ]
        for at in range(4):
            block = first + at
            rows = jnp.concatenate(
                [tile[at * PIECE : (at + 1) * PIECE, :] for tile in tiles], axis=0
            ).astype(jnp.bfloat16)
            full[block] = rows
            if block < blocks // 2:
                low[block] = rows
            else:
                high[block - blocks // 2] = rows


def packed_shapes(blocks):
    half = jax.ShapeDtypeStruct((blocks // 2, TILE, LANES), jnp.bfloat16)
    return (half, half, jax.ShapeDtypeStruct((blocks, TILE, LANES), jnp.bfloat16))


def norm_pack(own, z1, z2, z3, gain):
    blocks = own.shape[1] // LANES
    return pl.pallas_call(
        norm_pack_kernel,
        out_shape=packed_shapes(blocks),
        compiler_params=pltpu.CompilerParams(vmem_limit_bytes=8 * MIB),
        cost_estimate=pl.CostEstimate(flops=4_000_000, bytes_accessed=2_000_000, transcendentals=0),
    )(own, z1, z2, z3, gain[None, :])


def pack(own, z1, z2, z3):
    blocks = own.shape[0] // PIECE
    return pl.pallas_call(
        pack_kernel,
        out_shape=packed_shapes(blocks),
        compiler_params=pltpu.CompilerParams(vmem_limit_bytes=8 * MIB),
        cost_estimate=pl.CostEstimate(flops=1_000_000, bytes_accessed=2_000_000, transcendentals=0),
    )(own, z1, z2, z3)


def swapped(array, mask, devices):
    return lax.ppermute(array, "wide", [(i, i ^ mask) for i in range(devices)])


def gather_rows(piece, near, pack_pieces, devices):
    swap = functools.partial(swapped, devices=devices)
    z2, z3, z1 = swap(piece, 16), swap(piece, 24), swap(piece, 8)
    low, high, full = pack_pieces(near, z1, z2, z3)
    x_low, y_high = swap(low, 2), swap(high, 4)
    x_high, y_low = swap(high, 2), swap(low, 4)
    d_low, d_high = swap(x_low, 4), swap(y_high, 2)
    other = swap(full, 1)
    mine = [(low, high), (x_low, x_high), (y_low, y_high), (d_low, d_high)]
    theirs = [(swap(a, 1), swap(b, 1)) for a, b in mine[1:]]
    return mine, other, theirs


def prefetch_kernel(*refs):
    count = len(refs) // 3
    copies = [
        pltpu.make_async_copy(refs[at], refs[count + at], refs[2 * count + at]) for at in range(count)
    ]
    for copy in copies:
        copy.start()
    for copy in copies:
        copy.wait()


def prefetch(far, near=()):
    arrays = (*far, *near)
    return pl.pallas_call(
        prefetch_kernel,
        in_specs=[pl.BlockSpec(memory_space=pltpu.HBM)] * len(far)
        + [pl.BlockSpec(memory_space=pl.ANY)] * len(near),
        out_specs=[pl.BlockSpec(memory_space=pl.ANY)] * len(arrays),
        out_shape=[pltpu.VMEM(array.shape, array.dtype) for array in arrays],
        scratch_shapes=[pltpu.SemaphoreType.DMA] * len(arrays),
        compiler_params=pltpu.CompilerParams(vmem_limit_bytes=MIB),
        cost_estimate=pl.CostEstimate(
            flops=0,
            bytes_accessed=sum(array.size * array.dtype.itemsize for array in arrays),
            transcendentals=0,
        ),
    )(*[pltpu.with_memory_space_constraint(array, pltpu.HBM) for array in far], *near)


def source_rows(me, rows):
    at = lax.broadcasted_iota(jnp.int32, (1, rows), 1)
    core = at // (rows // 2)
    plane = (at // TILE) % 4
    column = (at // PIECE) % 4
    return (me ^ (core + 2 * plane + 8 * column)) * PIECE + at % PIECE


COUNT = 16


def multiply(refs, weight, total, weight_kv=None, total_kv=None):
    low, high = refs[0:8], refs[8:16]
    total[...] = jnp.zeros_like(total)
    if weight_kv is not None:
        total_kv[...] = jnp.zeros_like(total_kv)
    half = low[0].shape[0]
    blocks = 2 * half
    for parts, base in ((low, 0), (high, half)):

        def add(step, _, parts=parts, base=base):
            first = step * COUNT
            columns = []
            for at in range(COUNT):
                column = []
                for ref in parts:
                    offset = base if ref.shape[0] == blocks else 0
                    column.append(ref[first + at + offset])
                columns.append(jnp.concatenate(column, axis=0))
            rows = jnp.concatenate(columns, axis=1)
            depth = pl.ds(pl.multiple_of((base + first) * LANES, COUNT * LANES), COUNT * LANES)
            total[...] += jnp.dot(rows, weight[depth, :], preferred_element_type=jnp.float32)
            if weight_kv is not None:
                total_kv[...] += lax.dot_general(
                    rows, weight_kv[:, depth], (((1,), (1,)), ((), ())), preferred_element_type=jnp.float32
                )

        lax.fori_loop(0, half // COUNT, add, None)


def one_hot(equal):
    return equal.astype(jnp.float32).astype(jnp.bfloat16)


def as_column(row):
    count = row.shape[1]
    square = jnp.broadcast_to(row[...].astype(jnp.float32), (count, count))
    return jnp.transpose(square).astype(jnp.int32)


def query_kernel(*refs):
    weight, weight_kv, sessions, out, total, total_kv = refs[16:]
    me = lax.axis_index("wide")
    multiply(refs, weight, total, weight_kv, total_kv)
    rows, width = total.shape
    heads = width // LANES
    devices = rows // PIECE
    source = source_rows(me, rows)
    at = lax.broadcasted_iota(jnp.int32, (rows, rows), 0)
    session = jnp.sum(jnp.where(at == source, as_column(sessions), 0), axis=0, keepdims=True)
    stacked = jnp.concatenate(
        [total[:, h * LANES : (h + 1) * LANES].astype(jnp.bfloat16) for h in range(heads)], axis=0
    )
    codes = jnp.concatenate([session + h * rows for h in range(heads)], axis=1)
    at = lax.broadcasted_iota(jnp.int32, (rows * heads, rows * heads), 0)
    wanted = ((at // PIECE) % heads) * rows + (at // (PIECE * heads)) * PIECE + at % PIECE
    query = jnp.dot(one_hot(wanted == codes), stacked, preferred_element_type=jnp.float32)
    out[:, 0:TILE, :] = query.astype(jnp.bfloat16).reshape(devices, TILE, LANES)
    columns = total_kv.shape[1]
    at = lax.broadcasted_iota(jnp.int32, (devices * TILE, rows), 0)
    wanted = jnp.where(at % TILE < PIECE, (at // TILE) * PIECE + at % TILE, -1)
    keyval = total_kv[...].astype(jnp.bfloat16)
    ordered = jnp.dot(one_hot(wanted == session), keyval, preferred_element_type=jnp.float32)
    here = lax.broadcasted_iota(jnp.int32, (columns, LANES), 0)
    there = lax.broadcasted_iota(jnp.int32, (columns, LANES), 1)
    place = one_hot(there == here + (me % 2) * columns)
    placed = jnp.dot(ordered.astype(jnp.bfloat16), place, preferred_element_type=jnp.float32)
    out[:, TILE : 2 * TILE, :] = placed.astype(jnp.bfloat16).reshape(devices, TILE, LANES)


def out_kernel(*refs):
    weight, sessions, out, total = refs[16:]
    multiply(refs, weight, total)
    rows = total.shape[0]
    source = source_rows(lax.axis_index("wide"), rows)
    chosen = one_hot(as_column(sessions) == source)
    rounded = total[...].astype(jnp.bfloat16)
    out[...] = jnp.dot(chosen, rounded, preferred_element_type=jnp.float32).astype(jnp.bfloat16)


def gathered_operands(gathered):
    mine, other, theirs = gathered
    operands = []
    for half in range(2):
        operands += [pair[half] for pair in mine] + [other] + [pair[half] for pair in theirs]
    return operands


def project(kernel, gathered, weights, session_ids, out_shape, scratch):
    operands = gathered_operands(gathered) + list(weights) + [session_ids[None, :]]
    whole = pl.BlockSpec(memory_space=pltpu.VMEM)
    rows = session_ids.shape[0]
    depth = weights[0].shape[0]
    columns = sum(width for width in scratch)
    return pl.pallas_call(
        kernel,
        in_specs=[whole] * len(operands),
        out_specs=whole,
        out_shape=jax.ShapeDtypeStruct(out_shape, jnp.bfloat16),
        scratch_shapes=[pltpu.VMEM((rows, width), jnp.float32) for width in scratch],
        compiler_params=pltpu.CompilerParams(vmem_limit_bytes=PROJECT_MIB * MIB),
        cost_estimate=pl.CostEstimate(
            flops=2 * rows * depth * columns, bytes_accessed=2 * depth * (columns + rows), transcendentals=0
        ),
    )(*operands)


PROJECT_MIB = 8


def attend_kernel(received, keys, values, lengths, out):
    sessions, kv_heads, cache_len, width = keys.shape
    devices = received.shape[0]
    per_group = devices // kv_heads
    rows = per_group * TILE
    scale = width ** (-0.5)

    at = lax.broadcasted_iota(jnp.int32, (8, width), 0) % PIECE
    lane = lax.broadcasted_iota(jnp.int32, (8, width), 1)
    position = jnp.full((8, width), lengths[0], jnp.int32)
    for session in range(1, sessions):
        position = jnp.where(at == session, lengths[session], position)
    halfway = width // 2
    indices = (lane % halfway).astype(jnp.float32)
    inverse_freq = jnp.exp(indices * (-2.0 * math.log(ROPE_BASE) / width))
    angles = position.astype(jnp.float32) * inverse_freq
    cosine = jnp.cos(angles)
    sine = jnp.where(lane < halfway, -1.0, 1.0) * jnp.sin(angles)
    cosine = jnp.concatenate([cosine] * (rows // 8), axis=0)
    sine = jnp.concatenate([sine] * (rows // 8), axis=0)
    limits = jnp.concatenate(
        [jnp.full((1, cache_len), lengths[session], jnp.int32) for session in range(sessions)], axis=1
    )

    def rotate(vectors):
        return (vectors * cosine + pltpu.roll(vectors, halfway, 1) * sine).astype(jnp.bfloat16)

    own = received[:, TILE : 2 * TILE, :].astype(jnp.float32)
    pairs = devices // 2
    own = own.reshape(pairs, 2, TILE, width)
    own = own[:, 0] + own[:, 1]
    own = own[:, 0:8]
    own_rows = kv_heads * 8
    own_key = rotate(own[0:kv_heads].reshape(own_rows, width))
    own_value = own[kv_heads:].reshape(own_rows, width).astype(jnp.bfloat16)

    session = lax.broadcasted_iota(jnp.int32, (rows, sessions * cache_len), 0) % PIECE
    column = lax.broadcasted_iota(jnp.int32, (rows, sessions * cache_len), 1)
    valid = (column // cache_len == session) & (column % cache_len < limits)
    own_session = lax.broadcasted_iota(jnp.int32, (rows, own_rows), 0) % PIECE
    own_column = lax.broadcasted_iota(jnp.int32, (rows, own_rows), 1)
    for group in range(kv_heads):
        query = received[group * per_group : (group + 1) * per_group, 0:TILE, :]
        query = rotate(query.reshape(rows, width).astype(jnp.float32))
        group_keys = keys[:, group].reshape(sessions * cache_len, width)
        group_values = values[:, group].reshape(sessions * cache_len, width)
        contract = (((1,), (1,)), ((), ()))
        scores = (
            lax.dot_general(query, group_keys, contract, preferred_element_type=jnp.float32) * scale
        )
        scores = jnp.where(valid, scores, -jnp.inf)
        own_scores = (
            lax.dot_general(query, own_key, contract, preferred_element_type=jnp.float32) * scale
        )
        own_scores = jnp.where(own_column == group * 8 + own_session, own_scores, -jnp.inf)
        highest = jnp.maximum(
            jnp.max(scores, axis=-1, keepdims=True), jnp.max(own_scores, axis=-1, keepdims=True)
        )
        cached_exp = jnp.exp(scores - highest)
        own_exp = jnp.exp(own_scores - highest)
        total = jnp.sum(cached_exp, axis=-1, keepdims=True) + jnp.sum(
            own_exp, axis=-1, keepdims=True
        )
        weights = (cached_exp / total).astype(jnp.bfloat16)
        own_weights = (own_exp / total).astype(jnp.bfloat16)
        attended = jnp.dot(weights, group_values, preferred_element_type=jnp.float32)
        attended += jnp.dot(own_weights, own_value, preferred_element_type=jnp.float32)
        out[group * rows : (group + 1) * rows, :] = attended.astype(jnp.bfloat16)


def attend(received, keys, values, lengths):
    devices, _, width = received.shape
    whole = pl.BlockSpec(memory_space=pltpu.VMEM)
    return pl.pallas_call(
        attend_kernel,
        in_specs=[whole] * 3 + [pl.BlockSpec(memory_space=pltpu.SMEM)],
        out_shape=jax.ShapeDtypeStruct((devices * TILE, width), jnp.bfloat16),
        compiler_params=pltpu.CompilerParams(vmem_limit_bytes=8 * MIB),
        cost_estimate=pl.CostEstimate(
            flops=150_000_000, bytes_accessed=3_000_000, transcendentals=300_000
        ),
    )(received, keys, values, lengths)


def inside(array):
    return pltpu.with_memory_space_constraint(array, pltpu.VMEM)


def on_block(
    tokens, norm_gain, w_query, w_keyval, w_out, cache_keys, cache_values, session_ids, lengths, devices
):
    rows = devices * PIECE
    near, gain, near_query, near_keyval, near_keys, near_values = prefetch(
        (tokens, norm_gain, w_query, w_keyval, cache_keys, cache_values)
    )
    pack_tokens = functools.partial(norm_pack, gain=gain)
    gathered = gather_rows(tokens, near, pack_tokens, devices)
    local = project(
        query_kernel,
        gathered,
        (inside(near_query), inside(near_keyval)),
        session_ids,
        (devices, 2 * TILE, LANES),
        (w_query.shape[1], w_keyval.shape[0]),
    )
    received = lax.all_to_all(local, "wide", split_axis=0, concat_axis=0, tiled=True)
    attended = attend(received, inside(near_keys), inside(near_values), lengths)
    near_out, near = prefetch((w_out,), (attended,))
    gathered = gather_rows(attended, near, pack, devices)
    return project(
        out_kernel, gathered, (inside(near_out),), session_ids, (rows, w_out.shape[1]), (w_out.shape[1],)
    )


def fits_block(devices, tokens, w_query, w_keyval, cache_keys):
    sessions, kv_heads, cache_len, width = cache_keys.shape
    return (
        devices == 32
        and tokens.shape[0] == PIECE
        and sessions == PIECE
        and width == LANES
        and cache_len == LANES
        and kv_heads == KVH
        and w_query.shape[1] == 4 * LANES
        and w_keyval.shape[0] == LANES // 2
    )


def on_device(*args, devices):
    tokens, _, w_query, w_keyval, _, cache_keys = args[:6]
    if fits_block(devices, tokens, w_query, w_keyval, cache_keys):
        return on_block(*args, devices)
    return on_any(*args)


def solution(mesh):
    return jax.shard_map(
        functools.partial(on_device, devices=mesh.shape["wide"]),
        mesh=mesh,
        in_specs=(
            P(("groups", "wide"), None),
            P(),
            P(None, "wide"),
            P("wide", None),
            P(None, "wide"),
            P(("groups", "wide"), None, None, None),
            P(("groups", "wide"), None, None, None),
            P("groups"),
            P(("groups", "wide")),
        ),
        out_specs=P("groups", "wide"),
        check_vma=False,
    )
```

```python
import functools
import math

import jax
import jax.numpy as jnp
from jax import lax
from jax.experimental import pallas as pl
from jax.experimental.pallas import tpu as pltpu
from jax.sharding import PartitionSpec as P

HEADS = 128
KVH = 8


ROPE_BASE = 500000.0

LANES = 128
PIECE = 4
TILE = 16
MIB = 1 << 20


def rms_rows(rows, gain):
    values = rows.astype(jnp.float32)
    meansq = jnp.mean(values * values, axis=-1, keepdims=True)
    return (values * lax.rsqrt(meansq + 1e-05) * gain).astype(jnp.bfloat16)


def rotate_heads(values, positions):
    width = values.shape[-1]
    halfway = width // 2
    indices = jnp.arange(halfway).astype(jnp.float32)
    inverse_freq = jnp.exp(indices * (-2.0 * math.log(ROPE_BASE) / width))
    angles = positions.astype(jnp.float32)[:, None, None] * inverse_freq
    cosine = jnp.cos(angles)
    sine = jnp.sin(angles)
    first = values[..., :halfway]
    second = values[..., halfway:]
    return jnp.concatenate(
        [first * cosine - second * sine, second * cosine + first * sine], axis=-1
    )


def attend_sessions(query_sess, keyval_sess, cache_keys, cache_values, lengths):
    sessions = query_sess.shape[0]
    head_dim = query_sess.shape[1] // HEADS
    group = HEADS // KVH
    scale = head_dim ** (-0.5)
    rot_query = rotate_heads(
        query_sess.astype(jnp.float32).reshape(sessions, HEADS, head_dim), lengths
    )
    rot_query = rot_query.astype(jnp.bfloat16).reshape(sessions, KVH, group, head_dim)
    new_keys = keyval_sess[:, : KVH * head_dim].astype(jnp.float32).reshape(sessions, KVH, head_dim)
    own_key = rotate_heads(new_keys, lengths).astype(jnp.bfloat16)
    own_value = keyval_sess[:, KVH * head_dim :].reshape(sessions, KVH, head_dim)
    scores = (
        jnp.einsum("sgqd,sgpd->sgqp", rot_query, cache_keys, preferred_element_type=jnp.float32)
        * scale
    )
    valid = jnp.arange(cache_keys.shape[2])[None, :] < lengths[:, None]
    scores = jnp.where(valid[:, None, None, :], scores, -jnp.inf)
    own_score = (
        jnp.einsum("sgqd,sgd->sgq", rot_query, own_key, preferred_element_type=jnp.float32) * scale
    )
    highest = jnp.maximum(jnp.max(scores, axis=-1), own_score)
    cached_exp = jnp.exp(scores - highest[..., None])
    own_exp = jnp.exp(own_score - highest)
    total = jnp.sum(cached_exp, axis=-1) + own_exp
    cached_weight = (cached_exp / total[..., None]).astype(jnp.bfloat16)
    own_weight = (own_exp / total).astype(jnp.bfloat16)
    attended = jnp.einsum(
        "sgqp,sgpd->sgqd", cached_weight, cache_values, preferred_element_type=jnp.float32
    )
    attended = (
        attended
        + own_weight.astype(jnp.float32)[..., None] * own_value.astype(jnp.float32)[:, :, None, :]
    )
    return attended.reshape(sessions, HEADS * head_dim).astype(jnp.bfloat16)


def on_any(
    tokens, norm_gain, w_query, w_keyval, w_out, cache_keys, cache_values, session_ids, lengths
):
    normed = rms_rows(tokens, norm_gain)
    query_cols = w_query.shape[1]
    everyone = lax.all_gather(normed, "wide", axis=0, tiled=True)
    query_part = jnp.dot(everyone, w_query, preferred_element_type=jnp.float32).astype(jnp.bfloat16)
    keyval_part = lax.dot_general(
        everyone, w_keyval, (((1,), (1,)), ((), ())), preferred_element_type=jnp.float32
    ).astype(jnp.bfloat16)
    joined = jnp.concatenate([query_part, keyval_part], axis=1)
    inverse = jnp.argsort(session_ids)
    ordered = joined[inverse]
    query_local = ordered[:, :query_cols]
    keyval_local = ordered[:, query_cols:]
    query_sess, keyval_sess = (
        lax.all_to_all(query_local, "wide", split_axis=0, concat_axis=1, tiled=True),
        lax.all_to_all(keyval_local, "wide", split_axis=0, concat_axis=1, tiled=True),
    )
    attended = attend_sessions(query_sess, keyval_sess, cache_keys, cache_values, lengths)
    all_attended = lax.all_gather(attended, "wide", axis=0, tiled=True)
    out_sess = jnp.dot(all_attended, w_out, preferred_element_type=jnp.float32)
    return out_sess[session_ids].astype(jnp.bfloat16)


def norm_kernel(tokens, gain, main, rest):
    width = tokens.shape[1]
    values = tokens[...].astype(jnp.float32)
    meansq = jnp.sum(values * values, axis=-1, keepdims=True) * (1.0 / width)
    scale = lax.rsqrt(meansq + 1e-05)
    blocks = width // LANES
    split = main.shape[0] // PIECE
    for first in range(0, blocks, 4):
        tile = []
        for block in range(first, first + 4):
            lanes = slice(block * LANES, (block + 1) * LANES)
            tile.append(tokens[:, lanes].astype(jnp.float32) * scale * gain[:, lanes])
        tile = jnp.concatenate(tile, axis=0).astype(jnp.bfloat16)
        if first < split:
            main[first * PIECE : (first + 4) * PIECE, :] = tile
        else:
            rest[(first - split) * PIECE : (first - split + 4) * PIECE, :] = tile


def split_shapes(blocks):
    rest = blocks * 3 // 16
    return tuple(
        jax.ShapeDtypeStruct((count * PIECE, LANES), jnp.bfloat16) for count in (blocks - rest, rest)
    )


def norm(tokens, gain):
    return pl.pallas_call(
        norm_kernel,
        out_shape=split_shapes(tokens.shape[1] // LANES),
        compiler_params=pltpu.CompilerParams(vmem_limit_bytes=8 * MIB),
        cost_estimate=pl.CostEstimate(flops=500_000, bytes_accessed=400_000, transcendentals=0),
    )(
        pltpu.with_memory_space_constraint(tokens, pltpu.HBM),
        pltpu.with_memory_space_constraint(gain[None, :], pltpu.HBM),
    )


def pack_planes_kernel(*refs):
    pieces, out = refs[0], refs[-1]
    here = lax.axis_index("wide") // 2 % 4
    for first in range(0, out.shape[0], 4):
        tiles = [
            pieces[here ^ plane, first * PIECE : (first + 4) * PIECE, :].astype(jnp.float32)
            for plane in range(4)
        ]
        for at in range(4):
            rows = [tile[at * PIECE : (at + 1) * PIECE, :] for tile in tiles]
            out[first + at] = jnp.concatenate(rows, axis=0).astype(jnp.bfloat16)


def pack_planes(pieces, after):
    blocks = pieces.shape[1] // PIECE
    return pl.pallas_call(
        pack_planes_kernel,
        in_specs=[pl.BlockSpec(memory_space=pltpu.VMEM)] + [pl.BlockSpec(memory_space=pl.ANY)] * len(after),
        out_shape=jax.ShapeDtypeStruct((blocks, TILE, LANES), jnp.bfloat16),
        compiler_params=pltpu.CompilerParams(vmem_limit_bytes=8 * MIB),
        cost_estimate=pl.CostEstimate(flops=300_000, bytes_accessed=300_000, transcendentals=0),
    )(pieces, *after)


def pack_kernel(*refs, count, after):
    outs = refs[count + after :]
    blocks = outs[0].shape[0]
    held = blocks * PIECE
    pieces = [(ref, base) for ref in refs[:count] for base in range(0, ref.shape[0], held)]
    for first in range(0, blocks, 4):
        tiles = [
            ref[base + first * PIECE : base + (first + 4) * PIECE, :].astype(jnp.float32)
            for ref, base in pieces
        ]
        for at in range(4):
            block = first + at
            rows = jnp.concatenate(
                [tile[at * PIECE : (at + 1) * PIECE, :] for tile in tiles], axis=0
            ).astype(jnp.bfloat16)
            outs[0][block] = rows
            half = outs[1].shape[0]
            outs[1 + block // half][block % half] = rows


def pack(pieces, after):
    blocks = sum(piece.shape[0] for piece in pieces) // TILE
    counts = (blocks, blocks // 2, blocks // 2)
    return pl.pallas_call(
        functools.partial(pack_kernel, count=len(pieces), after=len(after)),
        in_specs=[pl.BlockSpec(memory_space=pltpu.VMEM)] * len(pieces)
        + [pl.BlockSpec(memory_space=pl.ANY)] * len(after),
        out_shape=[jax.ShapeDtypeStruct((count, TILE, LANES), jnp.bfloat16) for count in counts],
        compiler_params=pltpu.CompilerParams(vmem_limit_bytes=8 * MIB),
        cost_estimate=pl.CostEstimate(flops=1_000_000, bytes_accessed=1_000_000, transcendentals=0),
    )(*pieces, *after)


def swapped(array, mask, devices):
    return lax.ppermute(array, "wide", [(i, i ^ mask) for i in range(devices)])


def gather_rows(main, rest, devices, weights=()):
    swap = functools.partial(swapped, devices=devices)
    z1, z2, z3 = swap(main, 8), swap(main, 16), swap(main, 24)
    planes = [
        [first + 2 * plane for plane in range(4)] for first in range(devices) if first // 2 % 4 == 0
    ]
    rests = lax.all_gather(rest, "wide", axis_index_groups=planes)
    near_weights = prefetch(weights, ()) if weights else ()
    tail = pack_planes(rests, (z1, z2, z3, *near_weights[-1:]))
    tails = jnp.concatenate([tail, swap(tail, 8)], axis=0)
    full, low, high = pack((main, z1, z2, z3), near_weights[-1:])
    later_high, later_low, tails = lax.optimization_barrier((high, low, tails))
    x_low, y_high = swap(low, 2), swap(high, 4)
    x_high, y_low = swap(later_high, 2), swap(later_low, 4)
    d_low, d_high = swap(x_low, 4), swap(y_high, 2)
    x_high, y_low, full, near_tails, x_near, y_near = lax.optimization_barrier(
        (x_high, y_low, full, tails, x_low, y_high)
    )
    other = swap(full, 1)
    far_tails = swap(tails, 16)
    mine = [low, x_low, y_low, d_low, high, x_high, y_high, d_high]
    theirs = [other] + [swap(array, 1) for array in (x_near, y_low, d_low, x_high, y_near, d_high)]
    both = [tails, far_tails, swap(near_tails, 1), swap(far_tails, 1)]
    return mine + theirs + both, near_weights


RUNS = (
    ((0, 0), (1, 0), (2, 0), (3, 0), (8, 0), (9, 0), (10, 0), (11, 0)),
    ((4, 0), (5, 0), (6, 0), (7, 0), (8, 1), (12, 0), (13, 0), (14, 0)),
    ((15, 0), (15, 1), (16, 0), (16, 1), (17, 0), (17, 1), (18, 0), (18, 1)),
)
GATHERED = 19


def prefetch_kernel(*refs, count, after):
    outs, signals = refs[count + after : 2 * count + after], refs[2 * count + after :]
    copies = [
        pltpu.make_async_copy(refs[at], outs[at], signals[at]) for at in range(count)
    ]
    for copy in copies:
        copy.start()
    for copy in copies:
        copy.wait()


def prefetch(arrays, after):
    count = len(arrays)
    return pl.pallas_call(
        functools.partial(prefetch_kernel, count=count, after=len(after)),
        in_specs=[pl.BlockSpec(memory_space=pltpu.HBM)] * count
        + [pl.BlockSpec(memory_space=pl.ANY)] * len(after),
        out_specs=[pl.BlockSpec(memory_space=pl.ANY)] * count,
        out_shape=[pltpu.VMEM(array.shape, array.dtype) for array in arrays],
        scratch_shapes=[pltpu.SemaphoreType.DMA] * count,
        compiler_params=pltpu.CompilerParams(vmem_limit_bytes=MIB),
        cost_estimate=pl.CostEstimate(
            flops=0,
            bytes_accessed=sum(array.size * array.dtype.itemsize for array in arrays),
            transcendentals=0,
        ),
    )(*[pltpu.with_memory_space_constraint(array, pltpu.HBM) for array in arrays], *after)


def source_rows(me, rows):
    at = lax.broadcasted_iota(jnp.int32, (1, rows), 1)
    core = at // (rows // 2)
    plane = (at // TILE) % 4
    column = (at // PIECE) % 4
    return (me ^ (core + 2 * plane + 8 * column)) * PIECE + at % PIECE


MOST = 26


def multiply(refs, totals, rests):
    base = 0
    counts = (refs[0].shape[0], refs[4].shape[0], refs[15].shape[0] // 2)
    for run, count in enumerate(counts):
        steps = -(-count // MOST)
        width = count // steps
        parts = [(refs[at], offset * count) for at, offset in RUNS[run]]
        sums = rests if run == 2 else totals
        if run != 1:
            for total, _, _ in sums:
                total[...] = jnp.zeros_like(total)

        def add(step, _, parts=parts, base=base, width=width, sums=sums):
            first = step * width
            columns = []
            for at in range(width):
                columns.append(
                    jnp.concatenate([ref[first + at + offset] for ref, offset in parts], axis=0)
                )
            rows = jnp.concatenate(columns, axis=1)
            depth = pl.ds(pl.multiple_of((base + first) * LANES, 2 * LANES), width * LANES)
            for total, weight, turned in sums:
                if turned:
                    total[...] += lax.dot_general(
                        rows, weight[:, depth], (((1,), (1,)), ((), ())), preferred_element_type=jnp.float32
                    )
                else:
                    total[...] += jnp.dot(rows, weight[depth, :], preferred_element_type=jnp.float32)

        lax.fori_loop(0, steps, add, None)
        base += count
    for (total, _, _), (rest, _, _) in zip(totals, rests):
        for core in range(2):
            for plane in range(4):
                for pair in range(0, 4, 2):
                    low = core * 64 + plane * TILE + pair * PIECE
                    there = core * 64 + pair * TILE + plane * PIECE
                    total[low : low + 8, :] += jnp.concatenate(
                        [rest[there : there + 4, :], rest[there + TILE : there + TILE + 4, :]], axis=0
                    )


def one_hot(equal):
    return equal.astype(jnp.float32).astype(jnp.bfloat16)


def as_column(row):
    count = row.shape[1]
    square = jnp.broadcast_to(row[...].astype(jnp.float32), (count, count))
    return jnp.transpose(square).astype(jnp.int32)


def query_kernel(*refs):
    weight, weight_kv, sessions, out, total, total_kv, rest, rest_kv = refs[GATHERED:]
    me = lax.axis_index("wide")
    multiply(
        refs,
        ((total, weight, False), (total_kv, weight_kv, True)),
        ((rest, weight, False), (rest_kv, weight_kv, True)),
    )
    rows, width = total.shape
    heads = width // LANES
    devices = rows // PIECE
    source = source_rows(me, rows)
    at = lax.broadcasted_iota(jnp.int32, (rows, rows), 0)
    session = jnp.sum(jnp.where(at == source, as_column(sessions), 0), axis=0, keepdims=True)
    stacked = jnp.concatenate(
        [total[:, h * LANES : (h + 1) * LANES].astype(jnp.bfloat16) for h in range(heads)], axis=0
    )
    codes = jnp.concatenate([session + h * rows for h in range(heads)], axis=1)
    at = lax.broadcasted_iota(jnp.int32, (rows * heads, rows * heads), 0)
    wanted = ((at // PIECE) % heads) * rows + (at // (PIECE * heads)) * PIECE + at % PIECE
    query = jnp.dot(one_hot(wanted == codes), stacked, preferred_element_type=jnp.float32)
    out[:, 0:TILE, :] = query.astype(jnp.bfloat16).reshape(devices, TILE, LANES)
    columns = total_kv.shape[1]
    at = lax.broadcasted_iota(jnp.int32, (devices * TILE, rows), 0)
    wanted = jnp.where(at % TILE < PIECE, (at // TILE) * PIECE + at % TILE, -1)
    keyval = total_kv[...].astype(jnp.bfloat16)
    ordered = jnp.dot(one_hot(wanted == session), keyval, preferred_element_type=jnp.float32)
    here = lax.broadcasted_iota(jnp.int32, (columns, LANES), 0)
    there = lax.broadcasted_iota(jnp.int32, (columns, LANES), 1)
    place = one_hot(there == here + (me % 2) * columns)
    placed = jnp.dot(ordered.astype(jnp.bfloat16), place, preferred_element_type=jnp.float32)
    out[:, TILE : 2 * TILE, :] = placed.astype(jnp.bfloat16).reshape(devices, TILE, LANES)


def out_kernel(*refs):
    weight, sessions, out, total, rest = refs[GATHERED:]
    multiply(refs, ((total, weight, False),), ((rest, weight, False),))
    rows = total.shape[0]
    source = source_rows(lax.axis_index("wide"), rows)
    chosen = one_hot(as_column(sessions) == source)
    rounded = total[...].astype(jnp.bfloat16)
    out[...] = jnp.dot(chosen, rounded, preferred_element_type=jnp.float32).astype(jnp.bfloat16)


def project(kernel, gathered, weights, session_ids, out_shape, scratch):
    operands = list(gathered) + list(weights) + [session_ids[None, :]]
    whole = pl.BlockSpec(memory_space=pltpu.VMEM)
    rows = session_ids.shape[0]
    depth = weights[0].shape[0]
    columns = sum(width for width in scratch)
    return pl.pallas_call(
        kernel,
        in_specs=[whole] * len(operands),
        out_specs=whole,
        out_shape=jax.ShapeDtypeStruct(out_shape, jnp.bfloat16),
        scratch_shapes=[pltpu.VMEM((rows, width), jnp.float32) for width in 2 * scratch],
        compiler_params=pltpu.CompilerParams(vmem_limit_bytes=PROJECT_MIB * MIB),
        cost_estimate=pl.CostEstimate(
            flops=2 * rows * depth * columns, bytes_accessed=2 * depth * (columns + rows), transcendentals=0
        ),
    )(*operands)


PROJECT_MIB = 8


def attend_kernel(received, keys, values, lengths, main, rest):
    sessions, kv_heads, cache_len, width = keys.shape
    devices = received.shape[0]
    per_group = devices // kv_heads
    rows = per_group * TILE
    scale = width ** (-0.5)

    at = lax.broadcasted_iota(jnp.int32, (8, width), 0) % PIECE
    lane = lax.broadcasted_iota(jnp.int32, (8, width), 1)
    position = jnp.full((8, width), lengths[0], jnp.int32)
    for session in range(1, sessions):
        position = jnp.where(at == session, lengths[session], position)
    halfway = width // 2
    indices = (lane % halfway).astype(jnp.float32)
    inverse_freq = jnp.exp(indices * (-2.0 * math.log(ROPE_BASE) / width))
    angles = position.astype(jnp.float32) * inverse_freq
    cosine = jnp.cos(angles)
    sine = jnp.where(lane < halfway, -1.0, 1.0) * jnp.sin(angles)
    cosine = jnp.concatenate([cosine] * (rows // 8), axis=0)
    sine = jnp.concatenate([sine] * (rows // 8), axis=0)
    limits = jnp.concatenate(
        [jnp.full((1, cache_len), lengths[session], jnp.int32) for session in range(sessions)], axis=1
    )

    def rotate(vectors):
        return (vectors * cosine + pltpu.roll(vectors, halfway, 1) * sine).astype(jnp.bfloat16)

    own = received[:, TILE : 2 * TILE, :].astype(jnp.float32)
    pairs = devices // 2
    own = own.reshape(pairs, 2, TILE, width)
    own = own[:, 0] + own[:, 1]
    own = own[:, 0:8]
    own_rows = kv_heads * 8
    own_key = rotate(own[0:kv_heads].reshape(own_rows, width))
    own_value = own[kv_heads:].reshape(own_rows, width).astype(jnp.bfloat16)

    session = lax.broadcasted_iota(jnp.int32, (rows, sessions * cache_len), 0) % PIECE
    column = lax.broadcasted_iota(jnp.int32, (rows, sessions * cache_len), 1)
    valid = (column // cache_len == session) & (column % cache_len < limits)
    own_session = lax.broadcasted_iota(jnp.int32, (rows, own_rows), 0) % PIECE
    own_column = lax.broadcasted_iota(jnp.int32, (rows, own_rows), 1)
    for group in range(kv_heads):
        query = received[group * per_group : (group + 1) * per_group, 0:TILE, :]
        query = rotate(query.reshape(rows, width).astype(jnp.float32))
        group_keys = keys[:, group].reshape(sessions * cache_len, width)
        group_values = values[:, group].reshape(sessions * cache_len, width)
        contract = (((1,), (1,)), ((), ()))
        scores = (
            lax.dot_general(query, group_keys, contract, preferred_element_type=jnp.float32) * scale
        )
        scores = jnp.where(valid, scores, -jnp.inf)
        own_scores = (
            lax.dot_general(query, own_key, contract, preferred_element_type=jnp.float32) * scale
        )
        own_scores = jnp.where(own_column == group * 8 + own_session, own_scores, -jnp.inf)
        highest = jnp.maximum(
            jnp.max(scores, axis=-1, keepdims=True), jnp.max(own_scores, axis=-1, keepdims=True)
        )
        cached_exp = jnp.exp(scores - highest)
        own_exp = jnp.exp(own_scores - highest)
        total = jnp.sum(cached_exp, axis=-1, keepdims=True) + jnp.sum(
            own_exp, axis=-1, keepdims=True
        )
        weights = (cached_exp / total).astype(jnp.bfloat16)
        own_weights = (own_exp / total).astype(jnp.bfloat16)
        attended = jnp.dot(weights, group_values, preferred_element_type=jnp.float32)
        attended += jnp.dot(own_weights, own_value, preferred_element_type=jnp.float32)
        attended = attended.astype(jnp.bfloat16)
        first = group * rows
        kept = min(max(main.shape[0] - first, 0), rows)
        if kept:
            main[first : first + kept, :] = attended[0:kept, :]
        if kept < rows:
            first = max(first - main.shape[0], 0)
            rest[first : first + rows - kept, :] = attended[kept:, :]


def attend(received, keys, values, lengths):
    devices, _, width = received.shape
    whole = pl.BlockSpec(memory_space=pltpu.VMEM)
    return pl.pallas_call(
        attend_kernel,
        in_specs=[whole] * 3 + [pl.BlockSpec(memory_space=pltpu.SMEM)],
        out_shape=split_shapes(devices * TILE // PIECE),
        compiler_params=pltpu.CompilerParams(vmem_limit_bytes=8 * MIB),
        cost_estimate=pl.CostEstimate(
            flops=150_000_000, bytes_accessed=3_000_000, transcendentals=300_000
        ),
    )(received, keys, values, lengths)


def inside(array):
    return pltpu.with_memory_space_constraint(array, pltpu.VMEM)


def on_block(
    tokens, norm_gain, w_query, w_keyval, w_out, cache_keys, cache_values, session_ids, lengths, devices
):
    rows = devices * PIECE
    main, rest = norm(tokens, norm_gain)
    gathered, (near_query, near_keyval) = gather_rows(main, rest, devices, (w_query, w_keyval))
    local = project(
        query_kernel,
        gathered,
        (inside(near_query), inside(near_keyval)),
        session_ids,
        (devices, 2 * TILE, LANES),
        (w_query.shape[1], w_keyval.shape[0]),
    )
    received = lax.all_to_all(local, "wide", split_axis=0, concat_axis=0, tiled=True)
    main, rest = attend(received, inside(cache_keys), inside(cache_values), lengths)
    gathered, (near_out,) = gather_rows(main, rest, devices, (w_out,))
    return project(
        out_kernel, gathered, (inside(near_out),), session_ids, (rows, w_out.shape[1]), (w_out.shape[1],)
    )


def fits_block(devices, tokens, w_query, w_keyval, cache_keys):
    sessions, kv_heads, cache_len, width = cache_keys.shape
    return (
        devices == 32
        and tokens.shape[0] == PIECE
        and sessions == PIECE
        and width == LANES
        and cache_len == LANES
        and kv_heads == KVH
        and w_query.shape[1] == 4 * LANES
        and w_keyval.shape[0] == LANES // 2
    )


def on_device(*args, devices):
    tokens, _, w_query, w_keyval, _, cache_keys = args[:6]
    if fits_block(devices, tokens, w_query, w_keyval, cache_keys):
        return on_block(*args, devices)
    return on_any(*args)


def solution(mesh):
    return jax.shard_map(
        functools.partial(on_device, devices=mesh.shape["wide"]),
        mesh=mesh,
        in_specs=(
            P(("groups", "wide"), None),
            P(),
            P(None, "wide"),
            P("wide", None),
            P(None, "wide"),
            P(("groups", "wide"), None, None, None),
            P(("groups", "wide"), None, None, None),
            P("groups"),
            P(("groups", "wide")),
        ),
        out_specs=P("groups", "wide"),
        check_vma=False,
    )
```

```python
import functools
import math

import jax
import jax.numpy as jnp
from jax import lax
from jax.experimental import pallas as pl
from jax.experimental.pallas import tpu as pltpu
from jax.sharding import PartitionSpec as P

HEADS = 128
KVH = 8


ROPE_BASE = 500000.0

LANES = 128
PIECE = 4
TILE = 16
MIB = 1 << 20


def rms_rows(rows, gain):
    values = rows.astype(jnp.float32)
    meansq = jnp.mean(values * values, axis=-1, keepdims=True)
    return (values * lax.rsqrt(meansq + 1e-05) * gain).astype(jnp.bfloat16)


def rotate_heads(values, positions):
    width = values.shape[-1]
    halfway = width // 2
    indices = jnp.arange(halfway).astype(jnp.float32)
    inverse_freq = jnp.exp(indices * (-2.0 * math.log(ROPE_BASE) / width))
    angles = positions.astype(jnp.float32)[:, None, None] * inverse_freq
    cosine = jnp.cos(angles)
    sine = jnp.sin(angles)
    first = values[..., :halfway]
    second = values[..., halfway:]
    return jnp.concatenate(
        [first * cosine - second * sine, second * cosine + first * sine], axis=-1
    )


def attend_sessions(query_sess, keyval_sess, cache_keys, cache_values, lengths):
    sessions = query_sess.shape[0]
    head_dim = query_sess.shape[1] // HEADS
    group = HEADS // KVH
    scale = head_dim ** (-0.5)
    rot_query = rotate_heads(
        query_sess.astype(jnp.float32).reshape(sessions, HEADS, head_dim), lengths
    )
    rot_query = rot_query.astype(jnp.bfloat16).reshape(sessions, KVH, group, head_dim)
    new_keys = keyval_sess[:, : KVH * head_dim].astype(jnp.float32).reshape(sessions, KVH, head_dim)
    own_key = rotate_heads(new_keys, lengths).astype(jnp.bfloat16)
    own_value = keyval_sess[:, KVH * head_dim :].reshape(sessions, KVH, head_dim)
    scores = (
        jnp.einsum("sgqd,sgpd->sgqp", rot_query, cache_keys, preferred_element_type=jnp.float32)
        * scale
    )
    valid = jnp.arange(cache_keys.shape[2])[None, :] < lengths[:, None]
    scores = jnp.where(valid[:, None, None, :], scores, -jnp.inf)
    own_score = (
        jnp.einsum("sgqd,sgd->sgq", rot_query, own_key, preferred_element_type=jnp.float32) * scale
    )
    highest = jnp.maximum(jnp.max(scores, axis=-1), own_score)
    cached_exp = jnp.exp(scores - highest[..., None])
    own_exp = jnp.exp(own_score - highest)
    total = jnp.sum(cached_exp, axis=-1) + own_exp
    cached_weight = (cached_exp / total[..., None]).astype(jnp.bfloat16)
    own_weight = (own_exp / total).astype(jnp.bfloat16)
    attended = jnp.einsum(
        "sgqp,sgpd->sgqd", cached_weight, cache_values, preferred_element_type=jnp.float32
    )
    attended = (
        attended
        + own_weight.astype(jnp.float32)[..., None] * own_value.astype(jnp.float32)[:, :, None, :]
    )
    return attended.reshape(sessions, HEADS * head_dim).astype(jnp.bfloat16)


def on_any(
    tokens, norm_gain, w_query, w_keyval, w_out, cache_keys, cache_values, session_ids, lengths
):
    normed = rms_rows(tokens, norm_gain)
    query_cols = w_query.shape[1]
    everyone = lax.all_gather(normed, "wide", axis=0, tiled=True)
    query_part = jnp.dot(everyone, w_query, preferred_element_type=jnp.float32).astype(jnp.bfloat16)
    keyval_part = lax.dot_general(
        everyone, w_keyval, (((1,), (1,)), ((), ())), preferred_element_type=jnp.float32
    ).astype(jnp.bfloat16)
    joined = jnp.concatenate([query_part, keyval_part], axis=1)
    inverse = jnp.argsort(session_ids)
    ordered = joined[inverse]
    query_local = ordered[:, :query_cols]
    keyval_local = ordered[:, query_cols:]
    query_sess, keyval_sess = (
        lax.all_to_all(query_local, "wide", split_axis=0, concat_axis=1, tiled=True),
        lax.all_to_all(keyval_local, "wide", split_axis=0, concat_axis=1, tiled=True),
    )
    attended = attend_sessions(query_sess, keyval_sess, cache_keys, cache_values, lengths)
    all_attended = lax.all_gather(attended, "wide", axis=0, tiled=True)
    out_sess = jnp.dot(all_attended, w_out, preferred_element_type=jnp.float32)
    return out_sess[session_ids].astype(jnp.bfloat16)


def norm_pack_kernel(own, z1, z2, z3, gain, low, high, full):
    width = own.shape[1]
    blocks = width // LANES
    pieces = (own, z1, z2, z3)
    scales = []
    for piece in pieces:
        values = piece[...].astype(jnp.float32)
        meansq = jnp.sum(values * values, axis=-1, keepdims=True) * (1.0 / width)
        scales.append(lax.rsqrt(meansq + 1e-05))
    for block in range(blocks):
        lanes = slice(block * LANES, (block + 1) * LANES)
        factor = gain[:, lanes]
        rows = jnp.concatenate(
            [piece[:, lanes].astype(jnp.float32) * scale * factor for piece, scale in zip(pieces, scales)],
            axis=0,
        ).astype(jnp.bfloat16)
        full[block] = rows
        if block < blocks // 2:
            low[block] = rows
        else:
            high[block - blocks // 2] = rows


def pack_kernel(own, z1, z2, z3, low, high, full):
    blocks = own.shape[0] // PIECE
    pieces = (own, z1, z2, z3)
    for first in range(0, blocks, 4):
        tiles = [
            piece[first * PIECE : (first + 4) * PIECE, :].astype(jnp.float32) for piece in pieces
        ]
        for at in range(4):
            block = first + at
            rows = jnp.concatenate(
                [tile[at * PIECE : (at + 1) * PIECE, :] for tile in tiles], axis=0
            ).astype(jnp.bfloat16)
            full[block] = rows
            if block < blocks // 2:
                low[block] = rows
            else:
                high[block - blocks // 2] = rows


def packed_shapes(blocks):
    half = jax.ShapeDtypeStruct((blocks // 2, TILE, LANES), jnp.bfloat16)
    return (half, half, jax.ShapeDtypeStruct((blocks, TILE, LANES), jnp.bfloat16))


def norm_pack(own, z1, z2, z3, gain):
    blocks = own.shape[1] // LANES
    return pl.pallas_call(
        norm_pack_kernel,
        out_shape=packed_shapes(blocks),
        compiler_params=pltpu.CompilerParams(vmem_limit_bytes=8 * MIB),
        cost_estimate=pl.CostEstimate(flops=4_000_000, bytes_accessed=2_000_000, transcendentals=0),
    )(own, z1, z2, z3, gain[None, :])


def pack(own, z1, z2, z3):
    blocks = own.shape[0] // PIECE
    return pl.pallas_call(
        pack_kernel,
        out_shape=packed_shapes(blocks),
        compiler_params=pltpu.CompilerParams(vmem_limit_bytes=8 * MIB),
        cost_estimate=pl.CostEstimate(flops=1_000_000, bytes_accessed=2_000_000, transcendentals=0),
    )(own, z1, z2, z3)


def swapped(array, mask, devices):
    return lax.ppermute(array, "wide", [(i, i ^ mask) for i in range(devices)])


def gather_rows(piece, near, pack_pieces, devices):
    swap = functools.partial(swapped, devices=devices)
    z2, z3, z1 = swap(piece, 16), swap(piece, 24), swap(piece, 8)
    low, high, full = pack_pieces(near, z1, z2, z3)
    x_low, y_high = swap(low, 2), swap(high, 4)
    d_low, d_high = swap(x_low, 4), swap(y_high, 2)
    x_high, y_low = swap(high, 2), swap(low, 4)
    other = swap(full, 1)
    mine = [(low, high), (x_low, x_high), (y_low, y_high), (d_low, d_high)]
    theirs = [(swap(a, 1), swap(b, 1)) for a, b in mine[1:]]
    return mine, other, theirs


def prefetch_kernel(*refs):
    count = len(refs) // 3
    copies = [
        pltpu.make_async_copy(refs[at], refs[count + at], refs[2 * count + at]) for at in range(count)
    ]
    for copy in copies:
        copy.start()
    for copy in copies:
        copy.wait()


def prefetch(far, near=()):
    arrays = (*far, *near)
    return pl.pallas_call(
        prefetch_kernel,
        in_specs=[pl.BlockSpec(memory_space=pltpu.HBM)] * len(far)
        + [pl.BlockSpec(memory_space=pl.ANY)] * len(near),
        out_specs=[pl.BlockSpec(memory_space=pl.ANY)] * len(arrays),
        out_shape=[pltpu.VMEM(array.shape, array.dtype) for array in arrays],
        scratch_shapes=[pltpu.SemaphoreType.DMA] * len(arrays),
        compiler_params=pltpu.CompilerParams(vmem_limit_bytes=MIB),
        cost_estimate=pl.CostEstimate(
            flops=0,
            bytes_accessed=sum(array.size * array.dtype.itemsize for array in arrays),
            transcendentals=0,
        ),
    )(*[pltpu.with_memory_space_constraint(array, pltpu.HBM) for array in far], *near)


def source_rows(me, rows):
    at = lax.broadcasted_iota(jnp.int32, (1, rows), 1)
    core = at // (rows // 2)
    plane = (at // TILE) % 4
    column = (at // PIECE) % 4
    return (me ^ (core + 2 * plane + 8 * column)) * PIECE + at % PIECE


COUNT = 16


def multiply(refs, weight, total, weight_kv=None, total_kv=None):
    placed = [refs[ORDER.index(at)] for at in range(16)]
    low, high = placed[0:8], placed[8:16]
    total[...] = jnp.zeros_like(total)
    if weight_kv is not None:
        total_kv[...] = jnp.zeros_like(total_kv)
    half = low[0].shape[0]
    blocks = 2 * half
    for parts, base in ((low, 0), (high, half)):

        def add(step, _, parts=parts, base=base):
            first = step * COUNT
            columns = []
            for at in range(COUNT):
                column = []
                for ref in parts:
                    offset = base if ref.shape[0] == blocks else 0
                    column.append(ref[first + at + offset])
                columns.append(jnp.concatenate(column, axis=0))
            rows = jnp.concatenate(columns, axis=1)
            depth = pl.ds(pl.multiple_of((base + first) * LANES, COUNT * LANES), COUNT * LANES)
            total[...] += jnp.dot(rows, weight[depth, :], preferred_element_type=jnp.float32)
            if weight_kv is not None:
                total_kv[...] += lax.dot_general(
                    rows, weight_kv[:, depth], (((1,), (1,)), ((), ())), preferred_element_type=jnp.float32
                )

        lax.fori_loop(0, half // COUNT, add, None)


def one_hot(equal):
    return equal.astype(jnp.float32).astype(jnp.bfloat16)


def as_column(row):
    count = row.shape[1]
    square = jnp.broadcast_to(row[...].astype(jnp.float32), (count, count))
    return jnp.transpose(square).astype(jnp.int32)


def query_kernel(*refs):
    weight, weight_kv, sessions, out, total, total_kv = refs[16:]
    me = lax.axis_index("wide")
    multiply(refs, weight, total, weight_kv, total_kv)
    rows, width = total.shape
    heads = width // LANES
    devices = rows // PIECE
    source = source_rows(me, rows)
    at = lax.broadcasted_iota(jnp.int32, (rows, rows), 0)
    session = jnp.sum(jnp.where(at == source, as_column(sessions), 0), axis=0, keepdims=True)
    stacked = jnp.concatenate(
        [total[:, h * LANES : (h + 1) * LANES].astype(jnp.bfloat16) for h in range(heads)], axis=0
    )
    codes = jnp.concatenate([session + h * rows for h in range(heads)], axis=1)
    at = lax.broadcasted_iota(jnp.int32, (rows * heads, rows * heads), 0)
    wanted = ((at // PIECE) % heads) * rows + (at // (PIECE * heads)) * PIECE + at % PIECE
    query = jnp.dot(one_hot(wanted == codes), stacked, preferred_element_type=jnp.float32)
    out[:, 0:TILE, :] = query.astype(jnp.bfloat16).reshape(devices, TILE, LANES)
    columns = total_kv.shape[1]
    at = lax.broadcasted_iota(jnp.int32, (devices * TILE, rows), 0)
    wanted = jnp.where(at % TILE < PIECE, (at // TILE) * PIECE + at % TILE, -1)
    keyval = total_kv[...].astype(jnp.bfloat16)
    ordered = jnp.dot(one_hot(wanted == session), keyval, preferred_element_type=jnp.float32)
    here = lax.broadcasted_iota(jnp.int32, (columns, LANES), 0)
    there = lax.broadcasted_iota(jnp.int32, (columns, LANES), 1)
    place = one_hot(there == here + (me % 2) * columns)
    placed = jnp.dot(ordered.astype(jnp.bfloat16), place, preferred_element_type=jnp.float32)
    out[:, TILE : 2 * TILE, :] = placed.astype(jnp.bfloat16).reshape(devices, TILE, LANES)


def out_kernel(*refs):
    weight, sessions, out, total = refs[16:]
    multiply(refs, weight, total)
    rows = total.shape[0]
    source = source_rows(lax.axis_index("wide"), rows)
    chosen = one_hot(as_column(sessions) == source)
    rounded = total[...].astype(jnp.bfloat16)
    out[...] = jnp.dot(chosen, rounded, preferred_element_type=jnp.float32).astype(jnp.bfloat16)


ORDER = (3, 11, 7, 15, 0, 1, 8, 10, 2, 9, 4, 5, 6, 12, 13, 14)


def gathered_operands(gathered):
    mine, other, theirs = gathered
    operands = []
    for half in range(2):
        operands += [pair[half] for pair in mine] + [other] + [pair[half] for pair in theirs]
    return [operands[at] for at in ORDER]


def project(kernel, gathered, weights, session_ids, out_shape, scratch):
    operands = gathered_operands(gathered) + list(weights) + [session_ids[None, :]]
    whole = pl.BlockSpec(memory_space=pltpu.VMEM)
    rows = session_ids.shape[0]
    depth = weights[0].shape[0]
    columns = sum(width for width in scratch)
    return pl.pallas_call(
        kernel,
        in_specs=[whole] * len(operands),
        out_specs=whole,
        out_shape=jax.ShapeDtypeStruct(out_shape, jnp.bfloat16),
        scratch_shapes=[pltpu.VMEM((rows, width), jnp.float32) for width in scratch],
        compiler_params=pltpu.CompilerParams(vmem_limit_bytes=PROJECT_MIB * MIB),
        cost_estimate=pl.CostEstimate(
            flops=2 * rows * depth * columns, bytes_accessed=2 * depth * (columns + rows), transcendentals=0
        ),
    )(*operands)


PROJECT_MIB = 8


def attend_kernel(received, keys, values, lengths, out):
    sessions, kv_heads, cache_len, width = keys.shape
    devices = received.shape[0]
    per_group = devices // kv_heads
    rows = per_group * TILE
    scale = width ** (-0.5)

    at = lax.broadcasted_iota(jnp.int32, (8, width), 0) % PIECE
    lane = lax.broadcasted_iota(jnp.int32, (8, width), 1)
    position = jnp.full((8, width), lengths[0], jnp.int32)
    for session in range(1, sessions):
        position = jnp.where(at == session, lengths[session], position)
    halfway = width // 2
    indices = (lane % halfway).astype(jnp.float32)
    inverse_freq = jnp.exp(indices * (-2.0 * math.log(ROPE_BASE) / width))
    angles = position.astype(jnp.float32) * inverse_freq
    cosine = jnp.cos(angles)
    sine = jnp.where(lane < halfway, -1.0, 1.0) * jnp.sin(angles)
    cosine = jnp.concatenate([cosine] * (rows // 8), axis=0)
    sine = jnp.concatenate([sine] * (rows // 8), axis=0)
    limits = jnp.concatenate(
        [jnp.full((1, cache_len), lengths[session], jnp.int32) for session in range(sessions)], axis=1
    )

    def rotate(vectors):
        return (vectors * cosine + pltpu.roll(vectors, halfway, 1) * sine).astype(jnp.bfloat16)

    own = received[:, TILE : 2 * TILE, :].astype(jnp.float32)
    pairs = devices // 2
    own = own.reshape(pairs, 2, TILE, width)
    own = own[:, 0] + own[:, 1]
    own = own[:, 0:8]
    own_rows = kv_heads * 8
    own_key = rotate(own[0:kv_heads].reshape(own_rows, width))
    own_value = own[kv_heads:].reshape(own_rows, width).astype(jnp.bfloat16)

    session = lax.broadcasted_iota(jnp.int32, (rows, sessions * cache_len), 0) % PIECE
    column = lax.broadcasted_iota(jnp.int32, (rows, sessions * cache_len), 1)
    valid = (column // cache_len == session) & (column % cache_len < limits)
    own_session = lax.broadcasted_iota(jnp.int32, (rows, own_rows), 0) % PIECE
    own_column = lax.broadcasted_iota(jnp.int32, (rows, own_rows), 1)
    for group in range(kv_heads):
        query = received[group * per_group : (group + 1) * per_group, 0:TILE, :]
        query = rotate(query.reshape(rows, width).astype(jnp.float32))
        group_keys = keys[:, group].reshape(sessions * cache_len, width)
        group_values = values[:, group].reshape(sessions * cache_len, width)
        contract = (((1,), (1,)), ((), ()))
        scores = (
            lax.dot_general(query, group_keys, contract, preferred_element_type=jnp.float32) * scale
        )
        scores = jnp.where(valid, scores, -jnp.inf)
        own_scores = (
            lax.dot_general(query, own_key, contract, preferred_element_type=jnp.float32) * scale
        )
        own_scores = jnp.where(own_column == group * 8 + own_session, own_scores, -jnp.inf)
        highest = jnp.maximum(
            jnp.max(scores, axis=-1, keepdims=True), jnp.max(own_scores, axis=-1, keepdims=True)
        )
        cached_exp = jnp.exp(scores - highest)
        own_exp = jnp.exp(own_scores - highest)
        total = jnp.sum(cached_exp, axis=-1, keepdims=True) + jnp.sum(
            own_exp, axis=-1, keepdims=True
        )
        share = 1.0 / total
        weights = (cached_exp * share).astype(jnp.bfloat16)
        own_weights = (own_exp * share).astype(jnp.bfloat16)
        attended = jnp.dot(weights, group_values, preferred_element_type=jnp.float32)
        attended += jnp.dot(own_weights, own_value, preferred_element_type=jnp.float32)
        out[group * rows : (group + 1) * rows, :] = attended.astype(jnp.bfloat16)


def attend(received, keys, values, lengths):
    devices, _, width = received.shape
    whole = pl.BlockSpec(memory_space=pltpu.VMEM)
    return pl.pallas_call(
        attend_kernel,
        in_specs=[whole] * 3 + [pl.BlockSpec(memory_space=pltpu.SMEM)],
        out_shape=jax.ShapeDtypeStruct((devices * TILE, width), jnp.bfloat16),
        compiler_params=pltpu.CompilerParams(vmem_limit_bytes=8 * MIB),
        cost_estimate=pl.CostEstimate(
            flops=150_000_000, bytes_accessed=3_000_000, transcendentals=300_000
        ),
    )(received, keys, values, lengths)


def inside(array):
    return pltpu.with_memory_space_constraint(array, pltpu.VMEM)


def on_block(
    tokens, norm_gain, w_query, w_keyval, w_out, cache_keys, cache_values, session_ids, lengths, devices
):
    rows = devices * PIECE
    near, gain, near_query, near_keyval, near_keys, near_values = prefetch(
        (tokens, norm_gain, w_query, w_keyval, cache_keys, cache_values)
    )
    pack_tokens = functools.partial(norm_pack, gain=gain)
    gathered = gather_rows(tokens, near, pack_tokens, devices)
    local = project(
        query_kernel,
        gathered,
        (inside(near_query), inside(near_keyval)),
        session_ids,
        (devices, 2 * TILE, LANES),
        (w_query.shape[1], w_keyval.shape[0]),
    )
    received = lax.all_to_all(local, "wide", split_axis=0, concat_axis=0, tiled=True)
    attended = attend(received, inside(near_keys), inside(near_values), lengths)
    near_out, near = prefetch((w_out,), (attended,))
    gathered = gather_rows(attended, near, pack, devices)
    return project(
        out_kernel, gathered, (inside(near_out),), session_ids, (rows, w_out.shape[1]), (w_out.shape[1],)
    )


def fits_block(devices, tokens, w_query, w_keyval, cache_keys):
    sessions, kv_heads, cache_len, width = cache_keys.shape
    return (
        devices == 32
        and tokens.shape[0] == PIECE
        and sessions == PIECE
        and width == LANES
        and cache_len == LANES
        and kv_heads == KVH
        and w_query.shape[1] == 4 * LANES
        and w_keyval.shape[0] == LANES // 2
    )


def on_device(*args, devices):
    tokens, _, w_query, w_keyval, _, cache_keys = args[:6]
    if fits_block(devices, tokens, w_query, w_keyval, cache_keys):
        return on_block(*args, devices)
    return on_any(*args)


def solution(mesh):
    return jax.shard_map(
        functools.partial(on_device, devices=mesh.shape["wide"]),
        mesh=mesh,
        in_specs=(
            P(("groups", "wide"), None),
            P(),
            P(None, "wide"),
            P("wide", None),
            P(None, "wide"),
            P(("groups", "wide"), None, None, None),
            P(("groups", "wide"), None, None, None),
            P("groups"),
            P(("groups", "wide")),
        ),
        out_specs=P("groups", "wide"),
        check_vma=False,
    )
```

```python
import functools
import math

import jax
import jax.numpy as jnp
from jax import lax
from jax.experimental import pallas as pl
from jax.experimental.pallas import tpu as pltpu
from jax.sharding import PartitionSpec as P

HEADS = 128
KVH = 8


ROPE_BASE = 500000.0

LANES = 128
PIECE = 4
TILE = 16
EXTRA = 8
MIB = 1 << 20


def rms_rows(rows, gain):
    values = rows.astype(jnp.float32)
    meansq = jnp.mean(values * values, axis=-1, keepdims=True)
    return (values * lax.rsqrt(meansq + 1e-05) * gain).astype(jnp.bfloat16)


def rotate_heads(values, positions):
    width = values.shape[-1]
    halfway = width // 2
    indices = jnp.arange(halfway).astype(jnp.float32)
    inverse_freq = jnp.exp(indices * (-2.0 * math.log(ROPE_BASE) / width))
    angles = positions.astype(jnp.float32)[:, None, None] * inverse_freq
    cosine = jnp.cos(angles)
    sine = jnp.sin(angles)
    first = values[..., :halfway]
    second = values[..., halfway:]
    return jnp.concatenate(
        [first * cosine - second * sine, second * cosine + first * sine], axis=-1
    )


def attend_sessions(query_sess, keyval_sess, cache_keys, cache_values, lengths):
    sessions = query_sess.shape[0]
    head_dim = query_sess.shape[1] // HEADS
    group = HEADS // KVH
    scale = head_dim ** (-0.5)
    rot_query = rotate_heads(
        query_sess.astype(jnp.float32).reshape(sessions, HEADS, head_dim), lengths
    )
    rot_query = rot_query.astype(jnp.bfloat16).reshape(sessions, KVH, group, head_dim)
    new_keys = keyval_sess[:, : KVH * head_dim].astype(jnp.float32).reshape(sessions, KVH, head_dim)
    own_key = rotate_heads(new_keys, lengths).astype(jnp.bfloat16)
    own_value = keyval_sess[:, KVH * head_dim :].reshape(sessions, KVH, head_dim)
    scores = (
        jnp.einsum("sgqd,sgpd->sgqp", rot_query, cache_keys, preferred_element_type=jnp.float32)
        * scale
    )
    valid = jnp.arange(cache_keys.shape[2])[None, :] < lengths[:, None]
    scores = jnp.where(valid[:, None, None, :], scores, -jnp.inf)
    own_score = (
        jnp.einsum("sgqd,sgd->sgq", rot_query, own_key, preferred_element_type=jnp.float32) * scale
    )
    highest = jnp.maximum(jnp.max(scores, axis=-1), own_score)
    cached_exp = jnp.exp(scores - highest[..., None])
    own_exp = jnp.exp(own_score - highest)
    total = jnp.sum(cached_exp, axis=-1) + own_exp
    cached_weight = (cached_exp / total[..., None]).astype(jnp.bfloat16)
    own_weight = (own_exp / total).astype(jnp.bfloat16)
    attended = jnp.einsum(
        "sgqp,sgpd->sgqd", cached_weight, cache_values, preferred_element_type=jnp.float32
    )
    attended = (
        attended
        + own_weight.astype(jnp.float32)[..., None] * own_value.astype(jnp.float32)[:, :, None, :]
    )
    return attended.reshape(sessions, HEADS * head_dim).astype(jnp.bfloat16)


def on_any(
    tokens, norm_gain, w_query, w_keyval, w_out, cache_keys, cache_values, session_ids, lengths
):
    normed = rms_rows(tokens, norm_gain)
    query_cols = w_query.shape[1]
    everyone = lax.all_gather(normed, "wide", axis=0, tiled=True)
    query_part = jnp.dot(everyone, w_query, preferred_element_type=jnp.float32).astype(jnp.bfloat16)
    keyval_part = lax.dot_general(
        everyone, w_keyval, (((1,), (1,)), ((), ())), preferred_element_type=jnp.float32
    ).astype(jnp.bfloat16)
    joined = jnp.concatenate([query_part, keyval_part], axis=1)
    inverse = jnp.argsort(session_ids)
    ordered = joined[inverse]
    query_local = ordered[:, :query_cols]
    keyval_local = ordered[:, query_cols:]
    query_sess, keyval_sess = (
        lax.all_to_all(query_local, "wide", split_axis=0, concat_axis=1, tiled=True),
        lax.all_to_all(keyval_local, "wide", split_axis=0, concat_axis=1, tiled=True),
    )
    attended = attend_sessions(query_sess, keyval_sess, cache_keys, cache_values, lengths)
    all_attended = lax.all_gather(attended, "wide", axis=0, tiled=True)
    out_sess = jnp.dot(all_attended, w_out, preferred_element_type=jnp.float32)
    return out_sess[session_ids].astype(jnp.bfloat16)


def norm_pack_kernel(own, z1, z2, z3, gain, low, high, full):
    width = own.shape[1]
    blocks = width // LANES
    pieces = (own, z1, z2, z3)
    scales = []
    for piece in pieces:
        values = piece[...].astype(jnp.float32)
        meansq = jnp.sum(values * values, axis=-1, keepdims=True) * (1.0 / width)
        scales.append(lax.rsqrt(meansq + 1e-05))
    for block in range(blocks):
        lanes = slice(block * LANES, (block + 1) * LANES)
        factor = gain[:, lanes]
        rows = jnp.concatenate(
            [piece[:, lanes].astype(jnp.float32) * scale * factor for piece, scale in zip(pieces, scales)],
            axis=0,
        ).astype(jnp.bfloat16)
        full[block] = rows
        if block < blocks // 2:
            low[block] = rows
        else:
            high[block - blocks // 2] = rows


def pack_kernel(own, z1, z2, z3, low, high, full):
    blocks = own.shape[0] // PIECE
    pieces = (own, z1, z2, z3)
    for first in range(0, blocks, 4):
        tiles = [
            piece[first * PIECE : (first + 4) * PIECE, :].astype(jnp.float32) for piece in pieces
        ]
        for at in range(4):
            block = first + at
            rows = jnp.concatenate(
                [tile[at * PIECE : (at + 1) * PIECE, :] for tile in tiles], axis=0
            ).astype(jnp.bfloat16)
            full[block] = rows
            if block < blocks // 2:
                low[block] = rows
            else:
                high[block - blocks // 2] = rows


def packed_shapes(blocks):
    half = jax.ShapeDtypeStruct((blocks // 2, TILE, LANES), jnp.bfloat16)
    return (half, half, jax.ShapeDtypeStruct((blocks, TILE, LANES), jnp.bfloat16))


def norm_pack(own, z1, z2, z3, gain):
    blocks = own.shape[1] // LANES
    return pl.pallas_call(
        norm_pack_kernel,
        out_shape=packed_shapes(blocks),
        compiler_params=pltpu.CompilerParams(vmem_limit_bytes=8 * MIB),
        cost_estimate=pl.CostEstimate(flops=4_000_000, bytes_accessed=2_000_000, transcendentals=0),
    )(own, z1, z2, z3, gain[None, :])


def pack(own, z1, z2, z3):
    blocks = own.shape[0] // PIECE
    return pl.pallas_call(
        pack_kernel,
        out_shape=packed_shapes(blocks),
        compiler_params=pltpu.CompilerParams(vmem_limit_bytes=8 * MIB),
        cost_estimate=pl.CostEstimate(flops=1_000_000, bytes_accessed=2_000_000, transcendentals=0),
    )(own, z1, z2, z3)


def swapped(array, mask, devices):
    return lax.ppermute(array, "wide", [(i, i ^ mask) for i in range(devices)])


def gather_rows(piece, near, pack_pieces, devices):
    swap = functools.partial(swapped, devices=devices)
    z2, z3, z1 = swap(piece, 16), swap(piece, 24), swap(piece, 8)
    low, high, full = pack_pieces(near, z1, z2, z3)
    x_low, y_high = swap(low, 2), swap(high, 4)
    d_low, d_high = swap(x_low, 4), swap(y_high, 2)
    x_high, y_low = swap(high, 2), swap(low, 4)
    other = swap(full, 1)
    mine = [(low, high), (x_low, x_high), (y_low, y_high), (d_low, d_high)]
    theirs = [(swap(a, 1), swap(b, 1)) for a, b in mine[1:]]
    return mine, other, theirs


def prefetch_kernel(*refs):
    count = len(refs) // 3
    copies = [
        pltpu.make_async_copy(refs[at], refs[count + at], refs[2 * count + at]) for at in range(count)
    ]
    for copy in copies:
        copy.start()
    for copy in copies:
        copy.wait()


def prefetch(far, near=()):
    arrays = (*far, *near)
    return pl.pallas_call(
        prefetch_kernel,
        in_specs=[pl.BlockSpec(memory_space=pltpu.HBM)] * len(far)
        + [pl.BlockSpec(memory_space=pl.ANY)] * len(near),
        out_specs=[pl.BlockSpec(memory_space=pl.ANY)] * len(arrays),
        out_shape=[pltpu.VMEM(array.shape, array.dtype) for array in arrays],
        scratch_shapes=[pltpu.SemaphoreType.DMA] * len(arrays),
        compiler_params=pltpu.CompilerParams(vmem_limit_bytes=MIB),
        cost_estimate=pl.CostEstimate(
            flops=0,
            bytes_accessed=sum(array.size * array.dtype.itemsize for array in arrays),
            transcendentals=0,
        ),
    )(*[pltpu.with_memory_space_constraint(array, pltpu.HBM) for array in far], *near)


def source_rows(me, rows):
    at = lax.broadcasted_iota(jnp.int32, (1, rows), 1)
    core = at // (rows // 2)
    plane = (at // TILE) % 4
    column = (at // PIECE) % 4
    return (me ^ (core + 2 * plane + 8 * column)) * PIECE + at % PIECE


COUNT = 64


def multiply(refs, weight, total, weight_kv=None, total_kv=None):
    placed = [refs[ORDER.index(at)] for at in range(16)]
    low, high = placed[0:8], placed[8:16]
    total[...] = jnp.zeros_like(total)
    if weight_kv is not None:
        total_kv[...] = jnp.zeros_like(total_kv)
    half = low[0].shape[0]
    blocks = 2 * half
    for parts, base in ((low, 0), (high, half)):

        def add(step, _, parts=parts, base=base):
            first = step * COUNT
            columns = []
            for at in range(COUNT):
                column = []
                for ref in parts:
                    offset = base if ref.shape[0] == blocks else 0
                    column.append(ref[first + at + offset])
                columns.append(jnp.concatenate(column, axis=0))
            rows = jnp.concatenate(columns, axis=1)
            depth = pl.ds(pl.multiple_of((base + first) * LANES, COUNT * LANES), COUNT * LANES)
            total[...] += jnp.dot(rows, weight[depth, :], preferred_element_type=jnp.float32)
            if weight_kv is not None:
                total_kv[...] += lax.dot_general(
                    rows, weight_kv[:, depth], (((1,), (1,)), ((), ())), preferred_element_type=jnp.float32
                )

        lax.fori_loop(0, half // COUNT, add, None)


def one_hot(equal):
    return equal.astype(jnp.float32).astype(jnp.bfloat16)


def as_column(row):
    count = row.shape[1]
    square = jnp.broadcast_to(row[...].astype(jnp.float32), (count, count))
    return jnp.transpose(square).astype(jnp.int32)


def query_kernel(*refs):
    weight, weight_kv, sessions, out, total, total_kv = refs[16:]
    me = lax.axis_index("wide")
    multiply(refs, weight, total, weight_kv, total_kv)
    rows, width = total.shape
    heads = width // LANES
    devices = rows // PIECE
    source = source_rows(me, rows)
    at = lax.broadcasted_iota(jnp.int32, (rows, rows), 0)
    session = jnp.sum(jnp.where(at == source, as_column(sessions), 0), axis=0, keepdims=True)
    stacked = jnp.concatenate(
        [total[:, h * LANES : (h + 1) * LANES].astype(jnp.bfloat16) for h in range(heads)], axis=0
    )
    codes = jnp.concatenate([session + h * rows for h in range(heads)], axis=1)
    at = lax.broadcasted_iota(jnp.int32, (rows * heads, rows * heads), 0)
    wanted = ((at // PIECE) % heads) * rows + (at // (PIECE * heads)) * PIECE + at % PIECE
    query = jnp.dot(one_hot(wanted == codes), stacked, preferred_element_type=jnp.float32)
    out[:, 0:TILE, :] = query.astype(jnp.bfloat16).reshape(devices, TILE, LANES)
    columns = total_kv.shape[1]
    at = lax.broadcasted_iota(jnp.int32, (devices * EXTRA, rows), 0)
    wanted = jnp.where(at % EXTRA < PIECE, (at // EXTRA) * PIECE + at % EXTRA, -1)
    keyval = total_kv[...].astype(jnp.bfloat16)
    ordered = jnp.dot(one_hot(wanted == session), keyval, preferred_element_type=jnp.float32)
    here = lax.broadcasted_iota(jnp.int32, (columns, LANES), 0)
    there = lax.broadcasted_iota(jnp.int32, (columns, LANES), 1)
    place = one_hot(there == here + (me % 2) * columns)
    placed = jnp.dot(ordered.astype(jnp.bfloat16), place, preferred_element_type=jnp.float32)
    out[:, TILE : TILE + EXTRA, :] = placed.astype(jnp.bfloat16).reshape(devices, EXTRA, LANES)


def out_kernel(*refs):
    weight, sessions, out, total = refs[16:]
    multiply(refs, weight, total)
    rows = total.shape[0]
    source = source_rows(lax.axis_index("wide"), rows)
    chosen = one_hot(as_column(sessions) == source)
    rounded = total[...].astype(jnp.bfloat16)
    out[...] = jnp.dot(chosen, rounded, preferred_element_type=jnp.float32).astype(jnp.bfloat16)


ORDER = (3, 11, 7, 15, 0, 1, 8, 10, 2, 9, 4, 5, 6, 12, 13, 14)


def gathered_operands(gathered):
    mine, other, theirs = gathered
    operands = []
    for half in range(2):
        operands += [pair[half] for pair in mine] + [other] + [pair[half] for pair in theirs]
    return [operands[at] for at in ORDER]


def project(kernel, gathered, weights, session_ids, out_shape, scratch):
    operands = gathered_operands(gathered) + list(weights) + [session_ids[None, :]]
    whole = pl.BlockSpec(memory_space=pltpu.VMEM)
    rows = session_ids.shape[0]
    depth = weights[0].shape[0]
    columns = sum(width for width in scratch)
    return pl.pallas_call(
        kernel,
        in_specs=[whole] * len(operands),
        out_specs=whole,
        out_shape=jax.ShapeDtypeStruct(out_shape, jnp.bfloat16),
        scratch_shapes=[pltpu.VMEM((rows, width), jnp.float32) for width in scratch],
        compiler_params=pltpu.CompilerParams(vmem_limit_bytes=PROJECT_MIB * MIB),
        cost_estimate=pl.CostEstimate(
            flops=2 * rows * depth * columns, bytes_accessed=2 * depth * (columns + rows), transcendentals=0
        ),
    )(*operands)


PROJECT_MIB = 8


def attend_kernel(received, keys, values, lengths, out):
    sessions, kv_heads, cache_len, width = keys.shape
    devices = received.shape[0]
    per_group = devices // kv_heads
    rows = per_group * TILE
    scale = width ** (-0.5)

    at = lax.broadcasted_iota(jnp.int32, (8, width), 0) % PIECE
    lane = lax.broadcasted_iota(jnp.int32, (8, width), 1)
    position = jnp.full((8, width), lengths[0], jnp.int32)
    for session in range(1, sessions):
        position = jnp.where(at == session, lengths[session], position)
    halfway = width // 2
    indices = (lane % halfway).astype(jnp.float32)
    inverse_freq = jnp.exp(indices * (-2.0 * math.log(ROPE_BASE) / width))
    angles = position.astype(jnp.float32) * inverse_freq
    cosine = jnp.cos(angles)
    sine = jnp.where(lane < halfway, -1.0, 1.0) * jnp.sin(angles)
    cosine = jnp.concatenate([cosine] * (rows // 8), axis=0)
    sine = jnp.concatenate([sine] * (rows // 8), axis=0)
    limits = jnp.concatenate(
        [jnp.full((1, cache_len), lengths[session], jnp.int32) for session in range(sessions)], axis=1
    )

    def rotate(vectors):
        return (vectors * cosine + pltpu.roll(vectors, halfway, 1) * sine).astype(jnp.bfloat16)

    own = received[:, TILE : TILE + EXTRA, :].astype(jnp.float32)
    pairs = devices // 2
    own = own.reshape(pairs, 2, EXTRA, width)
    own = own[:, 0] + own[:, 1]
    own_rows = kv_heads * EXTRA
    own_key = rotate(own[0:kv_heads].reshape(own_rows, width))
    own_value = own[kv_heads:].reshape(own_rows, width).astype(jnp.bfloat16)

    session = lax.broadcasted_iota(jnp.int32, (rows, sessions * cache_len), 0) % PIECE
    column = lax.broadcasted_iota(jnp.int32, (rows, sessions * cache_len), 1)
    valid = (column // cache_len == session) & (column % cache_len < limits)
    own_session = lax.broadcasted_iota(jnp.int32, (rows, own_rows), 0) % PIECE
    own_column = lax.broadcasted_iota(jnp.int32, (rows, own_rows), 1)
    contract = (((1,), (1,)), ((), ()))
    for first in range(0, kv_heads, 8):
        groups = range(first, first + 8)
        queries = [
            rotate(
                received[group * per_group : (group + 1) * per_group, 0:TILE, :]
                .reshape(rows, width)
                .astype(jnp.float32)
            )
            for group in groups
        ]
        scores = [
            jnp.where(
                valid,
                lax.dot_general(
                    query,
                    keys[:, group].reshape(sessions * cache_len, width),
                    contract,
                    preferred_element_type=jnp.float32,
                )
                * scale,
                -jnp.inf,
            )
            for query, group in zip(queries, groups)
        ]
        own_scores = [
            jnp.where(
                own_column == group * EXTRA + own_session,
                lax.dot_general(query, own_key, contract, preferred_element_type=jnp.float32) * scale,
                -jnp.inf,
            )
            for query, group in zip(queries, groups)
        ]
        highest = [
            jnp.maximum(jnp.max(cached, axis=-1, keepdims=True), jnp.max(own, axis=-1, keepdims=True))
            for cached, own in zip(scores, own_scores)
        ]
        scores = [jnp.exp(cached - high) for cached, high in zip(scores, highest)]
        own_scores = [jnp.exp(own - high) for own, high in zip(own_scores, highest)]
        shares = [
            1.0 / (jnp.sum(cached, axis=-1, keepdims=True) + jnp.sum(own, axis=-1, keepdims=True))
            for cached, own in zip(scores, own_scores)
        ]
        for cached, own, share, group in zip(scores, own_scores, shares, groups):
            attended = jnp.dot(
                (cached * share).astype(jnp.bfloat16),
                values[:, group].reshape(sessions * cache_len, width),
                preferred_element_type=jnp.float32,
            )
            attended += jnp.dot(
                (own * share).astype(jnp.bfloat16), own_value, preferred_element_type=jnp.float32
            )
            out[group * rows : (group + 1) * rows, :] = attended.astype(jnp.bfloat16)


def attend(received, keys, values, lengths):
    devices, _, width = received.shape
    whole = pl.BlockSpec(memory_space=pltpu.VMEM)
    return pl.pallas_call(
        attend_kernel,
        in_specs=[whole] * 3 + [pl.BlockSpec(memory_space=pltpu.SMEM)],
        out_shape=jax.ShapeDtypeStruct((devices * TILE, width), jnp.bfloat16),
        compiler_params=pltpu.CompilerParams(vmem_limit_bytes=8 * MIB),
        cost_estimate=pl.CostEstimate(
            flops=150_000_000, bytes_accessed=3_000_000, transcendentals=300_000
        ),
    )(received, keys, values, lengths)


def inside(array):
    return pltpu.with_memory_space_constraint(array, pltpu.VMEM)


def on_block(
    tokens, norm_gain, w_query, w_keyval, w_out, cache_keys, cache_values, session_ids, lengths, devices
):
    rows = devices * PIECE
    near, gain, near_query, near_keyval, near_keys, near_values = prefetch(
        (tokens, norm_gain, w_query, w_keyval, cache_keys, cache_values)
    )
    pack_tokens = functools.partial(norm_pack, gain=gain)
    gathered = gather_rows(tokens, near, pack_tokens, devices)
    local = project(
        query_kernel,
        gathered,
        (inside(near_query), inside(near_keyval)),
        session_ids,
        (devices, TILE + EXTRA, LANES),
        (w_query.shape[1], w_keyval.shape[0]),
    )
    received = lax.all_to_all(local, "wide", split_axis=0, concat_axis=0, tiled=True)
    attended = attend(received, inside(near_keys), inside(near_values), lengths)
    near_out, near = prefetch((w_out,), (attended,))
    gathered = gather_rows(attended, near, pack, devices)
    return project(
        out_kernel, gathered, (inside(near_out),), session_ids, (rows, w_out.shape[1]), (w_out.shape[1],)
    )


def fits_block(devices, tokens, w_query, w_keyval, cache_keys):
    sessions, kv_heads, cache_len, width = cache_keys.shape
    return (
        devices == 32
        and tokens.shape[0] == PIECE
        and sessions == PIECE
        and width == LANES
        and cache_len == LANES
        and kv_heads == KVH
        and w_query.shape[1] == 4 * LANES
        and w_keyval.shape[0] == LANES // 2
    )


def on_device(*args, devices):
    tokens, _, w_query, w_keyval, _, cache_keys = args[:6]
    if fits_block(devices, tokens, w_query, w_keyval, cache_keys):
        return on_block(*args, devices)
    return on_any(*args)


def solution(mesh):
    return jax.shard_map(
        functools.partial(on_device, devices=mesh.shape["wide"]),
        mesh=mesh,
        in_specs=(
            P(("groups", "wide"), None),
            P(),
            P(None, "wide"),
            P("wide", None),
            P(None, "wide"),
            P(("groups", "wide"), None, None, None),
            P(("groups", "wide"), None, None, None),
            P("groups"),
            P(("groups", "wide")),
        ),
        out_specs=P("groups", "wide"),
        check_vma=False,
    )
```

```python
import functools
import math

import jax
import jax.numpy as jnp
from jax import lax
from jax.experimental import pallas as pl
from jax.experimental.pallas import tpu as pltpu
from jax.sharding import PartitionSpec as P

HEADS = 128
KVH = 8


ROPE_BASE = 500000.0

LANES = 128
PIECE = 4
TILE = 16
EXTRA = 8
MIB = 1 << 20


def rms_rows(rows, gain):
    values = rows.astype(jnp.float32)
    meansq = jnp.mean(values * values, axis=-1, keepdims=True)
    return (values * lax.rsqrt(meansq + 1e-05) * gain).astype(jnp.bfloat16)


def rotate_heads(values, positions):
    width = values.shape[-1]
    halfway = width // 2
    indices = jnp.arange(halfway).astype(jnp.float32)
    inverse_freq = jnp.exp(indices * (-2.0 * math.log(ROPE_BASE) / width))
    angles = positions.astype(jnp.float32)[:, None, None] * inverse_freq
    cosine = jnp.cos(angles)
    sine = jnp.sin(angles)
    first = values[..., :halfway]
    second = values[..., halfway:]
    return jnp.concatenate(
        [first * cosine - second * sine, second * cosine + first * sine], axis=-1
    )


def attend_sessions(query_sess, keyval_sess, cache_keys, cache_values, lengths):
    sessions = query_sess.shape[0]
    head_dim = query_sess.shape[1] // HEADS
    group = HEADS // KVH
    scale = head_dim ** (-0.5)
    rot_query = rotate_heads(
        query_sess.astype(jnp.float32).reshape(sessions, HEADS, head_dim), lengths
    )
    rot_query = rot_query.astype(jnp.bfloat16).reshape(sessions, KVH, group, head_dim)
    new_keys = keyval_sess[:, : KVH * head_dim].astype(jnp.float32).reshape(sessions, KVH, head_dim)
    own_key = rotate_heads(new_keys, lengths).astype(jnp.bfloat16)
    own_value = keyval_sess[:, KVH * head_dim :].reshape(sessions, KVH, head_dim)
    scores = (
        jnp.einsum("sgqd,sgpd->sgqp", rot_query, cache_keys, preferred_element_type=jnp.float32)
        * scale
    )
    valid = jnp.arange(cache_keys.shape[2])[None, :] < lengths[:, None]
    scores = jnp.where(valid[:, None, None, :], scores, -jnp.inf)
    own_score = (
        jnp.einsum("sgqd,sgd->sgq", rot_query, own_key, preferred_element_type=jnp.float32) * scale
    )
    highest = jnp.maximum(jnp.max(scores, axis=-1), own_score)
    cached_exp = jnp.exp(scores - highest[..., None])
    own_exp = jnp.exp(own_score - highest)
    total = jnp.sum(cached_exp, axis=-1) + own_exp
    cached_weight = (cached_exp / total[..., None]).astype(jnp.bfloat16)
    own_weight = (own_exp / total).astype(jnp.bfloat16)
    attended = jnp.einsum(
        "sgqp,sgpd->sgqd", cached_weight, cache_values, preferred_element_type=jnp.float32
    )
    attended = (
        attended
        + own_weight.astype(jnp.float32)[..., None] * own_value.astype(jnp.float32)[:, :, None, :]
    )
    return attended.reshape(sessions, HEADS * head_dim).astype(jnp.bfloat16)


def on_any(
    tokens, norm_gain, w_query, w_keyval, w_out, cache_keys, cache_values, session_ids, lengths
):
    normed = rms_rows(tokens, norm_gain)
    query_cols = w_query.shape[1]
    everyone = lax.all_gather(normed, "wide", axis=0, tiled=True)
    query_part = jnp.dot(everyone, w_query, preferred_element_type=jnp.float32).astype(jnp.bfloat16)
    keyval_part = lax.dot_general(
        everyone, w_keyval, (((1,), (1,)), ((), ())), preferred_element_type=jnp.float32
    ).astype(jnp.bfloat16)
    joined = jnp.concatenate([query_part, keyval_part], axis=1)
    inverse = jnp.argsort(session_ids)
    ordered = joined[inverse]
    query_local = ordered[:, :query_cols]
    keyval_local = ordered[:, query_cols:]
    query_sess, keyval_sess = (
        lax.all_to_all(query_local, "wide", split_axis=0, concat_axis=1, tiled=True),
        lax.all_to_all(keyval_local, "wide", split_axis=0, concat_axis=1, tiled=True),
    )
    attended = attend_sessions(query_sess, keyval_sess, cache_keys, cache_values, lengths)
    all_attended = lax.all_gather(attended, "wide", axis=0, tiled=True)
    out_sess = jnp.dot(all_attended, w_out, preferred_element_type=jnp.float32)
    return out_sess[session_ids].astype(jnp.bfloat16)


def norm_pack_kernel(own, z1, z2, z3, gain, low, high, full):
    width = own.shape[1]
    blocks = width // LANES
    pieces = (own, z1, z2, z3)
    scales = []
    for piece in pieces:
        values = piece[...].astype(jnp.float32)
        meansq = jnp.sum(values * values, axis=-1, keepdims=True) * (1.0 / width)
        scales.append(lax.rsqrt(meansq + 1e-05))
    for block in range(blocks):
        lanes = slice(block * LANES, (block + 1) * LANES)
        factor = gain[:, lanes]
        rows = jnp.concatenate(
            [piece[:, lanes].astype(jnp.float32) * scale * factor for piece, scale in zip(pieces, scales)],
            axis=0,
        ).astype(jnp.bfloat16)
        full[block] = rows
        if block < blocks // 2:
            low[block] = rows
        else:
            high[block - blocks // 2] = rows


def pack_kernel(own, z1, z2, z3, low, high, full):
    blocks = own.shape[0] // PIECE
    pieces = (own, z1, z2, z3)
    for first in range(0, blocks, 4):
        tiles = [
            piece[first * PIECE : (first + 4) * PIECE, :].astype(jnp.float32) for piece in pieces
        ]
        for at in range(4):
            block = first + at
            rows = jnp.concatenate(
                [tile[at * PIECE : (at + 1) * PIECE, :] for tile in tiles], axis=0
            ).astype(jnp.bfloat16)
            full[block] = rows
            if block < blocks // 2:
                low[block] = rows
            else:
                high[block - blocks // 2] = rows


def packed_shapes(blocks):
    half = jax.ShapeDtypeStruct((blocks // 2, TILE, LANES), jnp.bfloat16)
    return (half, half, jax.ShapeDtypeStruct((blocks, TILE, LANES), jnp.bfloat16))


def norm_pack(own, z1, z2, z3, gain):
    blocks = own.shape[1] // LANES
    return pl.pallas_call(
        norm_pack_kernel,
        out_shape=packed_shapes(blocks),
        compiler_params=pltpu.CompilerParams(vmem_limit_bytes=8 * MIB),
        cost_estimate=pl.CostEstimate(flops=4_000_000, bytes_accessed=2_000_000, transcendentals=0),
    )(own, z1, z2, z3, gain[None, :])


def pack(own, z1, z2, z3):
    blocks = own.shape[0] // PIECE
    return pl.pallas_call(
        pack_kernel,
        out_shape=packed_shapes(blocks),
        compiler_params=pltpu.CompilerParams(vmem_limit_bytes=8 * MIB),
        cost_estimate=pl.CostEstimate(flops=1_000_000, bytes_accessed=2_000_000, transcendentals=0),
    )(own, z1, z2, z3)


def swapped(array, mask, devices):
    return lax.ppermute(array, "wide", [(i, i ^ mask) for i in range(devices)])


def gather_rows(piece, near, pack_pieces, devices):
    swap = functools.partial(swapped, devices=devices)
    z2, z3, z1 = swap(piece, 16), swap(piece, 24), swap(piece, 8)
    low, high, full = pack_pieces(near, z1, z2, z3)
    x_low, y_high = swap(low, 2), swap(high, 4)
    d_low, d_high = swap(x_low, 4), swap(y_high, 2)
    x_high, y_low = swap(high, 2), swap(low, 4)
    other = swap(full, 1)
    mine = [(low, high), (x_low, x_high), (y_low, y_high), (d_low, d_high)]
    theirs = [(swap(a, 1), swap(b, 1)) for a, b in mine[1:]]
    return mine, other, theirs


def prefetch_kernel(*refs):
    count = len(refs) // 3
    copies = [
        pltpu.make_async_copy(refs[at], refs[count + at], refs[2 * count + at]) for at in range(count)
    ]
    for copy in copies:
        copy.start()
    for copy in copies:
        copy.wait()


def prefetch(far, near=()):
    arrays = (*far, *near)
    return pl.pallas_call(
        prefetch_kernel,
        in_specs=[pl.BlockSpec(memory_space=pltpu.HBM)] * len(far)
        + [pl.BlockSpec(memory_space=pl.ANY)] * len(near),
        out_specs=[pl.BlockSpec(memory_space=pl.ANY)] * len(arrays),
        out_shape=[pltpu.VMEM(array.shape, array.dtype) for array in arrays],
        scratch_shapes=[pltpu.SemaphoreType.DMA] * len(arrays),
        compiler_params=pltpu.CompilerParams(vmem_limit_bytes=MIB),
        cost_estimate=pl.CostEstimate(
            flops=0,
            bytes_accessed=sum(array.size * array.dtype.itemsize for array in arrays),
            transcendentals=0,
        ),
    )(*[pltpu.with_memory_space_constraint(array, pltpu.HBM) for array in far], *near)


def source_rows(me, rows):
    at = lax.broadcasted_iota(jnp.int32, (1, rows), 1)
    core = at // (rows // 2)
    plane = (at // TILE) % 4
    column = (at // PIECE) % 4
    return (me ^ (core + 2 * plane + 8 * column)) * PIECE + at % PIECE


def multiply(refs, weight, weight_kv=None):
    placed = [refs[ORDER.index(at)] for at in range(16)]
    half = placed[0].shape[0]
    total = total_kv = 0.0
    for parts, base in ((placed[0:8], 0), (placed[8:16], half)):
        columns = []
        for at in range(half):
            column = [ref[at + (base if ref.shape[0] > half else 0)] for ref in parts]
            columns.append(jnp.concatenate(column, axis=0))
        rows = jnp.concatenate(columns, axis=1)
        depth = slice(base * LANES, (base + half) * LANES)
        total += jnp.dot(rows, weight[depth, :], preferred_element_type=jnp.float32)
        if weight_kv is not None:
            total_kv += lax.dot_general(
                rows, weight_kv[:, depth], (((1,), (1,)), ((), ())), preferred_element_type=jnp.float32
            )
    return total, total_kv


def one_hot(equal):
    return equal.astype(jnp.float32).astype(jnp.bfloat16)


def as_column(row):
    count = row.shape[1]
    square = jnp.broadcast_to(row[...].astype(jnp.float32), (count, count))
    return jnp.transpose(square).astype(jnp.int32)


def query_kernel(*refs):
    weight, weight_kv, sessions, out = refs[16:]
    me = lax.axis_index("wide")
    total, total_kv = multiply(refs, weight, weight_kv)
    rows, width = total.shape
    heads = width // LANES
    devices = rows // PIECE
    source = source_rows(me, rows)
    at = lax.broadcasted_iota(jnp.int32, (rows, rows), 0)
    session = jnp.sum(jnp.where(at == source, as_column(sessions), 0), axis=0, keepdims=True)
    stacked = jnp.concatenate(
        [total[:, h * LANES : (h + 1) * LANES].astype(jnp.bfloat16) for h in range(heads)], axis=0
    )
    codes = jnp.concatenate([session + h * rows for h in range(heads)], axis=1)
    at = lax.broadcasted_iota(jnp.int32, (rows * heads, rows * heads), 0)
    wanted = ((at // PIECE) % heads) * rows + (at // (PIECE * heads)) * PIECE + at % PIECE
    query = jnp.dot(one_hot(wanted == codes), stacked, preferred_element_type=jnp.float32)
    out[:, 0:TILE, :] = query.astype(jnp.bfloat16).reshape(devices, TILE, LANES)
    columns = total_kv.shape[1]
    at = lax.broadcasted_iota(jnp.int32, (devices * EXTRA, rows), 0)
    wanted = jnp.where(at % EXTRA < PIECE, (at // EXTRA) * PIECE + at % EXTRA, -1)
    keyval = total_kv.astype(jnp.bfloat16)
    ordered = jnp.dot(one_hot(wanted == session), keyval, preferred_element_type=jnp.float32)
    here = lax.broadcasted_iota(jnp.int32, (columns, LANES), 0)
    there = lax.broadcasted_iota(jnp.int32, (columns, LANES), 1)
    place = one_hot(there == here + (me % 2) * columns)
    placed = jnp.dot(ordered.astype(jnp.bfloat16), place, preferred_element_type=jnp.float32)
    out[:, TILE : TILE + EXTRA, :] = placed.astype(jnp.bfloat16).reshape(devices, EXTRA, LANES)


def out_kernel(*refs):
    weight, sessions, out = refs[16:]
    total, _ = multiply(refs, weight)
    rows = total.shape[0]
    source = source_rows(lax.axis_index("wide"), rows)
    chosen = one_hot(as_column(sessions) == source)
    rounded = total.astype(jnp.bfloat16)
    out[...] = jnp.dot(chosen, rounded, preferred_element_type=jnp.float32).astype(jnp.bfloat16)


ORDER = (3, 11, 7, 15, 0, 1, 8, 10, 2, 9, 4, 5, 6, 12, 13, 14)


def gathered_operands(gathered):
    mine, other, theirs = gathered
    operands = []
    for half in range(2):
        operands += [pair[half] for pair in mine] + [other] + [pair[half] for pair in theirs]
    return [operands[at] for at in ORDER]


def project(kernel, gathered, weights, session_ids, out_shape, columns):
    operands = gathered_operands(gathered) + list(weights) + [session_ids[None, :]]
    whole = pl.BlockSpec(memory_space=pltpu.VMEM)
    rows = session_ids.shape[0]
    depth = weights[0].shape[0]
    return pl.pallas_call(
        kernel,
        in_specs=[whole] * len(operands),
        out_specs=whole,
        out_shape=jax.ShapeDtypeStruct(out_shape, jnp.bfloat16),
        compiler_params=pltpu.CompilerParams(vmem_limit_bytes=PROJECT_MIB * MIB),
        cost_estimate=pl.CostEstimate(
            flops=2 * rows * depth * columns, bytes_accessed=2 * depth * (columns + rows), transcendentals=0
        ),
    )(*operands)


PROJECT_MIB = 8


def attend_kernel(received, keys, values, lengths, out):
    sessions, kv_heads, cache_len, width = keys.shape
    devices = received.shape[0]
    per_group = devices // kv_heads
    rows = per_group * TILE
    scale = width ** (-0.5)

    at = lax.broadcasted_iota(jnp.int32, (8, width), 0) % PIECE
    lane = lax.broadcasted_iota(jnp.int32, (8, width), 1)
    position = jnp.full((8, width), lengths[0], jnp.int32)
    for session in range(1, sessions):
        position = jnp.where(at == session, lengths[session], position)
    halfway = width // 2
    indices = (lane % halfway).astype(jnp.float32)
    inverse_freq = jnp.exp(indices * (-2.0 * math.log(ROPE_BASE) / width))
    angles = position.astype(jnp.float32) * inverse_freq
    cosine = jnp.cos(angles)
    sine = jnp.where(lane < halfway, -1.0, 1.0) * jnp.sin(angles)
    cosine = jnp.concatenate([cosine] * (rows // 8), axis=0)
    sine = jnp.concatenate([sine] * (rows // 8), axis=0)
    limits = jnp.concatenate(
        [jnp.full((1, cache_len), lengths[session], jnp.int32) for session in range(sessions)], axis=1
    )

    def rotate(vectors):
        return (vectors * cosine + pltpu.roll(vectors, halfway, 1) * sine).astype(jnp.bfloat16)

    own = received[:, TILE : TILE + EXTRA, :].astype(jnp.float32)
    pairs = devices // 2
    own = own.reshape(pairs, 2, EXTRA, width)
    own = own[:, 0] + own[:, 1]
    own_rows = kv_heads * EXTRA
    own_key = rotate(own[0:kv_heads].reshape(own_rows, width))
    own_value = own[kv_heads:].reshape(own_rows, width).astype(jnp.bfloat16)

    session = lax.broadcasted_iota(jnp.int32, (rows, sessions * cache_len), 0) % PIECE
    column = lax.broadcasted_iota(jnp.int32, (rows, sessions * cache_len), 1)
    valid = (column // cache_len == session) & (column % cache_len < limits)
    own_session = lax.broadcasted_iota(jnp.int32, (rows, own_rows), 0) % PIECE
    own_column = lax.broadcasted_iota(jnp.int32, (rows, own_rows), 1)
    contract = (((1,), (1,)), ((), ()))
    for first in range(0, kv_heads, 8):
        groups = range(first, first + 8)
        queries = [
            rotate(
                received[group * per_group : (group + 1) * per_group, 0:TILE, :]
                .reshape(rows, width)
                .astype(jnp.float32)
            )
            for group in groups
        ]
        scores = [
            jnp.where(
                valid,
                lax.dot_general(
                    query,
                    keys[:, group].reshape(sessions * cache_len, width),
                    contract,
                    preferred_element_type=jnp.float32,
                )
                * scale,
                -jnp.inf,
            )
            for query, group in zip(queries, groups)
        ]
        own_scores = [
            jnp.where(
                own_column == group * EXTRA + own_session,
                lax.dot_general(query, own_key, contract, preferred_element_type=jnp.float32) * scale,
                -jnp.inf,
            )
            for query, group in zip(queries, groups)
        ]
        highest = [
            jnp.maximum(jnp.max(cached, axis=-1, keepdims=True), jnp.max(own, axis=-1, keepdims=True))
            for cached, own in zip(scores, own_scores)
        ]
        scores = [jnp.exp(cached - high) for cached, high in zip(scores, highest)]
        own_scores = [jnp.exp(own - high) for own, high in zip(own_scores, highest)]
        shares = [
            1.0 / (jnp.sum(cached, axis=-1, keepdims=True) + jnp.sum(own, axis=-1, keepdims=True))
            for cached, own in zip(scores, own_scores)
        ]
        for cached, own, share, group in zip(scores, own_scores, shares, groups):
            attended = jnp.dot(
                (cached * share).astype(jnp.bfloat16),
                values[:, group].reshape(sessions * cache_len, width),
                preferred_element_type=jnp.float32,
            )
            attended += jnp.dot(
                (own * share).astype(jnp.bfloat16), own_value, preferred_element_type=jnp.float32
            )
            out[group * rows : (group + 1) * rows, :] = attended.astype(jnp.bfloat16)


def attend(received, keys, values, lengths):
    devices, _, width = received.shape
    whole = pl.BlockSpec(memory_space=pltpu.VMEM)
    return pl.pallas_call(
        attend_kernel,
        in_specs=[whole] * 3 + [pl.BlockSpec(memory_space=pltpu.SMEM)],
        out_shape=jax.ShapeDtypeStruct((devices * TILE, width), jnp.bfloat16),
        compiler_params=pltpu.CompilerParams(vmem_limit_bytes=8 * MIB),
        cost_estimate=pl.CostEstimate(
            flops=150_000_000, bytes_accessed=3_000_000, transcendentals=300_000
        ),
    )(received, keys, values, lengths)


def inside(array):
    return pltpu.with_memory_space_constraint(array, pltpu.VMEM)


def on_block(
    tokens, norm_gain, w_query, w_keyval, w_out, cache_keys, cache_values, session_ids, lengths, devices
):
    rows = devices * PIECE
    near, gain, near_query, near_keyval, near_keys, near_values = prefetch(
        (tokens, norm_gain, w_query, w_keyval, cache_keys, cache_values)
    )
    pack_tokens = functools.partial(norm_pack, gain=gain)
    gathered = gather_rows(tokens, near, pack_tokens, devices)
    local = project(
        query_kernel,
        gathered,
        (inside(near_query), inside(near_keyval)),
        session_ids,
        (devices, TILE + EXTRA, LANES),
        w_query.shape[1] + w_keyval.shape[0],
    )
    received = lax.all_to_all(local, "wide", split_axis=0, concat_axis=0, tiled=True)
    attended = attend(received, inside(near_keys), inside(near_values), lengths)
    near_out, near = prefetch((w_out,), (attended,))
    gathered = gather_rows(attended, near, pack, devices)
    return project(
        out_kernel, gathered, (inside(near_out),), session_ids, (rows, w_out.shape[1]), w_out.shape[1]
    )


def fits_block(devices, tokens, w_query, w_keyval, cache_keys):
    sessions, kv_heads, cache_len, width = cache_keys.shape
    return (
        devices == 32
        and tokens.shape[0] == PIECE
        and sessions == PIECE
        and width == LANES
        and cache_len == LANES
        and kv_heads == KVH
        and w_query.shape[1] == 4 * LANES
        and w_keyval.shape[0] == LANES // 2
    )


def on_device(*args, devices):
    tokens, _, w_query, w_keyval, _, cache_keys = args[:6]
    if fits_block(devices, tokens, w_query, w_keyval, cache_keys):
        return on_block(*args, devices)
    return on_any(*args)


def solution(mesh):
    return jax.shard_map(
        functools.partial(on_device, devices=mesh.shape["wide"]),
        mesh=mesh,
        in_specs=(
            P(("groups", "wide"), None),
            P(),
            P(None, "wide"),
            P("wide", None),
            P(None, "wide"),
            P(("groups", "wide"), None, None, None),
            P(("groups", "wide"), None, None, None),
            P("groups"),
            P(("groups", "wide")),
        ),
        out_specs=P("groups", "wide"),
        check_vma=False,
    )
```

```python
import functools
import math

import jax
import jax.numpy as jnp
from jax import lax
from jax.experimental import pallas as pl
from jax.experimental.pallas import tpu as pltpu
from jax.sharding import PartitionSpec as P

HEADS = 128
KVH = 8


ROPE_BASE = 500000.0

LANES = 128
PIECE = 4
TILE = 16
EXTRA = 8
MIB = 1 << 20


def rms_rows(rows, gain):
    values = rows.astype(jnp.float32)
    meansq = jnp.mean(values * values, axis=-1, keepdims=True)
    return (values * lax.rsqrt(meansq + 1e-05) * gain).astype(jnp.bfloat16)


def rotate_heads(values, positions):
    width = values.shape[-1]
    halfway = width // 2
    indices = jnp.arange(halfway).astype(jnp.float32)
    inverse_freq = jnp.exp(indices * (-2.0 * math.log(ROPE_BASE) / width))
    angles = positions.astype(jnp.float32)[:, None, None] * inverse_freq
    cosine = jnp.cos(angles)
    sine = jnp.sin(angles)
    first = values[..., :halfway]
    second = values[..., halfway:]
    return jnp.concatenate(
        [first * cosine - second * sine, second * cosine + first * sine], axis=-1
    )


def attend_sessions(query_sess, keyval_sess, cache_keys, cache_values, lengths):
    sessions = query_sess.shape[0]
    head_dim = query_sess.shape[1] // HEADS
    group = HEADS // KVH
    scale = head_dim ** (-0.5)
    rot_query = rotate_heads(
        query_sess.astype(jnp.float32).reshape(sessions, HEADS, head_dim), lengths
    )
    rot_query = rot_query.astype(jnp.bfloat16).reshape(sessions, KVH, group, head_dim)
    new_keys = keyval_sess[:, : KVH * head_dim].astype(jnp.float32).reshape(sessions, KVH, head_dim)
    own_key = rotate_heads(new_keys, lengths).astype(jnp.bfloat16)
    own_value = keyval_sess[:, KVH * head_dim :].reshape(sessions, KVH, head_dim)
    scores = (
        jnp.einsum("sgqd,sgpd->sgqp", rot_query, cache_keys, preferred_element_type=jnp.float32)
        * scale
    )
    valid = jnp.arange(cache_keys.shape[2])[None, :] < lengths[:, None]
    scores = jnp.where(valid[:, None, None, :], scores, -jnp.inf)
    own_score = (
        jnp.einsum("sgqd,sgd->sgq", rot_query, own_key, preferred_element_type=jnp.float32) * scale
    )
    highest = jnp.maximum(jnp.max(scores, axis=-1), own_score)
    cached_exp = jnp.exp(scores - highest[..., None])
    own_exp = jnp.exp(own_score - highest)
    total = jnp.sum(cached_exp, axis=-1) + own_exp
    cached_weight = (cached_exp / total[..., None]).astype(jnp.bfloat16)
    own_weight = (own_exp / total).astype(jnp.bfloat16)
    attended = jnp.einsum(
        "sgqp,sgpd->sgqd", cached_weight, cache_values, preferred_element_type=jnp.float32
    )
    attended = (
        attended
        + own_weight.astype(jnp.float32)[..., None] * own_value.astype(jnp.float32)[:, :, None, :]
    )
    return attended.reshape(sessions, HEADS * head_dim).astype(jnp.bfloat16)


def on_any(
    tokens, norm_gain, w_query, w_keyval, w_out, cache_keys, cache_values, session_ids, lengths
):
    normed = rms_rows(tokens, norm_gain)
    query_cols = w_query.shape[1]
    everyone = lax.all_gather(normed, "wide", axis=0, tiled=True)
    query_part = jnp.dot(everyone, w_query, preferred_element_type=jnp.float32).astype(jnp.bfloat16)
    keyval_part = lax.dot_general(
        everyone, w_keyval, (((1,), (1,)), ((), ())), preferred_element_type=jnp.float32
    ).astype(jnp.bfloat16)
    joined = jnp.concatenate([query_part, keyval_part], axis=1)
    inverse = jnp.argsort(session_ids)
    ordered = joined[inverse]
    query_local = ordered[:, :query_cols]
    keyval_local = ordered[:, query_cols:]
    query_sess, keyval_sess = (
        lax.all_to_all(query_local, "wide", split_axis=0, concat_axis=1, tiled=True),
        lax.all_to_all(keyval_local, "wide", split_axis=0, concat_axis=1, tiled=True),
    )
    attended = attend_sessions(query_sess, keyval_sess, cache_keys, cache_values, lengths)
    all_attended = lax.all_gather(attended, "wide", axis=0, tiled=True)
    out_sess = jnp.dot(all_attended, w_out, preferred_element_type=jnp.float32)
    return out_sess[session_ids].astype(jnp.bfloat16)


def norm_pack_kernel(own, z1, z2, z3, gain, low, high, full):
    width = own.shape[1]
    blocks = width // LANES
    pieces = (own, z1, z2, z3)
    scales = []
    for piece in pieces:
        values = piece[...].astype(jnp.float32)
        meansq = jnp.sum(values * values, axis=-1, keepdims=True) * (1.0 / width)
        scales.append(lax.rsqrt(meansq + 1e-05))
    for block in range(blocks):
        lanes = slice(block * LANES, (block + 1) * LANES)
        factor = gain[:, lanes]
        rows = jnp.concatenate(
            [piece[:, lanes].astype(jnp.float32) * scale * factor for piece, scale in zip(pieces, scales)],
            axis=0,
        ).astype(jnp.bfloat16)
        full[block] = rows
        if block < blocks // 2:
            low[block] = rows
        else:
            high[block - blocks // 2] = rows


def pack_kernel(own, z1, z2, z3, low, high, full):
    blocks = own.shape[0] // PIECE
    pieces = (own, z1, z2, z3)
    for first in range(0, blocks, 4):
        tiles = [
            piece[first * PIECE : (first + 4) * PIECE, :].astype(jnp.float32) for piece in pieces
        ]
        for at in range(4):
            block = first + at
            rows = jnp.concatenate(
                [tile[at * PIECE : (at + 1) * PIECE, :] for tile in tiles], axis=0
            ).astype(jnp.bfloat16)
            full[block] = rows
            if block < blocks // 2:
                low[block] = rows
            else:
                high[block - blocks // 2] = rows


def packed_shapes(blocks):
    half = jax.ShapeDtypeStruct((blocks // 2, TILE, LANES), jnp.bfloat16)
    return (half, half, jax.ShapeDtypeStruct((blocks, TILE, LANES), jnp.bfloat16))


def norm_pack(own, z1, z2, z3, gain):
    blocks = own.shape[1] // LANES
    return pl.pallas_call(
        norm_pack_kernel,
        out_shape=packed_shapes(blocks),
        compiler_params=pltpu.CompilerParams(vmem_limit_bytes=8 * MIB),
        cost_estimate=pl.CostEstimate(flops=4_000_000, bytes_accessed=2_000_000, transcendentals=0),
    )(own, z1, z2, z3, gain[None, :])


def pack(own, z1, z2, z3):
    blocks = own.shape[0] // PIECE
    return pl.pallas_call(
        pack_kernel,
        out_shape=packed_shapes(blocks),
        compiler_params=pltpu.CompilerParams(vmem_limit_bytes=8 * MIB),
        cost_estimate=pl.CostEstimate(flops=1_000_000, bytes_accessed=2_000_000, transcendentals=0),
    )(own, z1, z2, z3)


def swapped(array, mask, devices):
    return lax.ppermute(array, "wide", [(i, i ^ mask) for i in range(devices)])


def gather_rows(piece, near, pack_pieces, devices):
    swap = functools.partial(swapped, devices=devices)
    z2, z3, z1 = swap(piece, 16), swap(piece, 24), swap(piece, 8)
    low, high, full = pack_pieces(near, z1, z2, z3)
    x_low, y_high = swap(low, 2), swap(high, 4)
    d_low, d_high = swap(x_low, 4), swap(y_high, 2)
    x_high, y_low = swap(high, 2), swap(low, 4)
    other = swap(full, 1)
    mine = [(low, high), (x_low, x_high), (y_low, y_high), (d_low, d_high)]
    other, x_late, y_late = lax.optimization_barrier((other, x_high, y_low))
    theirs = [
        (swap(x_low, 1), swap(x_late, 1)),
        (swap(y_late, 1), swap(y_high, 1)),
        (swap(d_low, 1), swap(d_high, 1)),
    ]
    return mine, other, theirs


def prefetch_kernel(*refs):
    count = len(refs) // 3
    copies = [
        pltpu.make_async_copy(refs[at], refs[count + at], refs[2 * count + at]) for at in range(count)
    ]
    for copy in copies:
        copy.start()
    for copy in copies:
        copy.wait()


def prefetch(far, near=()):
    arrays = (*far, *near)
    return pl.pallas_call(
        prefetch_kernel,
        in_specs=[pl.BlockSpec(memory_space=pltpu.HBM)] * len(far)
        + [pl.BlockSpec(memory_space=pl.ANY)] * len(near),
        out_specs=[pl.BlockSpec(memory_space=pl.ANY)] * len(arrays),
        out_shape=[pltpu.VMEM(array.shape, array.dtype) for array in arrays],
        scratch_shapes=[pltpu.SemaphoreType.DMA] * len(arrays),
        compiler_params=pltpu.CompilerParams(vmem_limit_bytes=MIB),
        cost_estimate=pl.CostEstimate(
            flops=0,
            bytes_accessed=sum(array.size * array.dtype.itemsize for array in arrays),
            transcendentals=0,
        ),
    )(*[pltpu.with_memory_space_constraint(array, pltpu.HBM) for array in far], *near)


def source_rows(me, rows):
    at = lax.broadcasted_iota(jnp.int32, (1, rows), 1)
    core = at // (rows // 2)
    plane = (at // TILE) % 4
    column = (at // PIECE) % 4
    return (me ^ (core + 2 * plane + 8 * column)) * PIECE + at % PIECE


COUNT = 64


def multiply(refs, weight, total, weight_kv=None, total_kv=None):
    placed = [refs[ORDER.index(at)] for at in range(16)]
    low, high = placed[0:8], placed[8:16]
    total[...] = jnp.zeros_like(total)
    if weight_kv is not None:
        total_kv[...] = jnp.zeros_like(total_kv)
    half = low[0].shape[0]
    blocks = 2 * half
    for parts, base in ((low, 0), (high, half)):

        def add(step, _, parts=parts, base=base):
            first = step * COUNT
            columns = []
            for at in range(COUNT):
                column = []
                for ref in parts:
                    offset = base if ref.shape[0] == blocks else 0
                    column.append(ref[first + at + offset])
                columns.append(jnp.concatenate(column, axis=0))
            rows = jnp.concatenate(columns, axis=1)
            depth = pl.ds(pl.multiple_of((base + first) * LANES, COUNT * LANES), COUNT * LANES)
            total[...] += jnp.dot(rows, weight[depth, :], preferred_element_type=jnp.float32)
            if weight_kv is not None:
                total_kv[...] += lax.dot_general(
                    rows, weight_kv[:, depth], (((1,), (1,)), ((), ())), preferred_element_type=jnp.float32
                )

        lax.fori_loop(0, half // COUNT, add, None)


def one_hot(equal):
    return equal.astype(jnp.float32).astype(jnp.bfloat16)


def as_column(row):
    count = row.shape[1]
    square = jnp.broadcast_to(row[...].astype(jnp.float32), (count, count))
    return jnp.transpose(square).astype(jnp.int32)


def query_kernel(*refs):
    weight, weight_kv, sessions, out, total, total_kv = refs[16:]
    me = lax.axis_index("wide")
    multiply(refs, weight, total, weight_kv, total_kv)
    rows, width = total.shape
    heads = width // LANES
    devices = rows // PIECE
    source = source_rows(me, rows)
    at = lax.broadcasted_iota(jnp.int32, (rows, rows), 0)
    session = jnp.sum(jnp.where(at == source, as_column(sessions), 0), axis=0, keepdims=True)
    stacked = jnp.concatenate(
        [total[:, h * LANES : (h + 1) * LANES].astype(jnp.bfloat16) for h in range(heads)], axis=0
    )
    codes = jnp.concatenate([session + h * rows for h in range(heads)], axis=1)
    at = lax.broadcasted_iota(jnp.int32, (rows * heads, rows * heads), 0)
    wanted = ((at // PIECE) % heads) * rows + (at // (PIECE * heads)) * PIECE + at % PIECE
    query = jnp.dot(one_hot(wanted == codes), stacked, preferred_element_type=jnp.float32)
    out[:, 0:TILE, :] = query.astype(jnp.bfloat16).reshape(devices, TILE, LANES)
    columns = total_kv.shape[1]
    at = lax.broadcasted_iota(jnp.int32, (devices * EXTRA, rows), 0)
    wanted = jnp.where(at % EXTRA < PIECE, (at // EXTRA) * PIECE + at % EXTRA, -1)
    keyval = total_kv[...].astype(jnp.bfloat16)
    ordered = jnp.dot(one_hot(wanted == session), keyval, preferred_element_type=jnp.float32)
    here = lax.broadcasted_iota(jnp.int32, (columns, LANES), 0)
    there = lax.broadcasted_iota(jnp.int32, (columns, LANES), 1)
    place = one_hot(there == here + (me % 2) * columns)
    placed = jnp.dot(ordered.astype(jnp.bfloat16), place, preferred_element_type=jnp.float32)
    out[:, TILE : TILE + EXTRA, :] = placed.astype(jnp.bfloat16).reshape(devices, EXTRA, LANES)


def out_kernel(*refs):
    weight, sessions, out, total = refs[16:]
    multiply(refs, weight, total)
    rows = total.shape[0]
    source = source_rows(lax.axis_index("wide"), rows)
    chosen = one_hot(as_column(sessions) == source)
    rounded = total[...].astype(jnp.bfloat16)
    out[...] = jnp.dot(chosen, rounded, preferred_element_type=jnp.float32).astype(jnp.bfloat16)


ORDER = (3, 11, 7, 15, 0, 1, 8, 10, 2, 9, 4, 5, 6, 12, 13, 14)


def gathered_operands(gathered):
    mine, other, theirs = gathered
    operands = []
    for half in range(2):
        operands += [pair[half] for pair in mine] + [other] + [pair[half] for pair in theirs]
    return [operands[at] for at in ORDER]


def project(kernel, gathered, weights, session_ids, out_shape, scratch):
    operands = gathered_operands(gathered) + list(weights) + [session_ids[None, :]]
    whole = pl.BlockSpec(memory_space=pltpu.VMEM)
    rows = session_ids.shape[0]
    depth = weights[0].shape[0]
    columns = sum(width for width in scratch)
    return pl.pallas_call(
        kernel,
        in_specs=[whole] * len(operands),
        out_specs=whole,
        out_shape=jax.ShapeDtypeStruct(out_shape, jnp.bfloat16),
        scratch_shapes=[pltpu.VMEM((rows, width), jnp.float32) for width in scratch],
        compiler_params=pltpu.CompilerParams(vmem_limit_bytes=PROJECT_MIB * MIB),
        cost_estimate=pl.CostEstimate(
            flops=2 * rows * depth * columns, bytes_accessed=2 * depth * (columns + rows), transcendentals=0
        ),
    )(*operands)


PROJECT_MIB = 8


def attend_kernel(received, keys, values, lengths, out):
    sessions, kv_heads, cache_len, width = keys.shape
    devices = received.shape[0]
    per_group = devices // kv_heads
    rows = per_group * TILE
    scale = width ** (-0.5)

    at = lax.broadcasted_iota(jnp.int32, (8, width), 0) % PIECE
    lane = lax.broadcasted_iota(jnp.int32, (8, width), 1)
    position = jnp.full((8, width), lengths[0], jnp.int32)
    for session in range(1, sessions):
        position = jnp.where(at == session, lengths[session], position)
    halfway = width // 2
    indices = (lane % halfway).astype(jnp.float32)
    inverse_freq = jnp.exp(indices * (-2.0 * math.log(ROPE_BASE) / width))
    angles = position.astype(jnp.float32) * inverse_freq
    cosine = jnp.cos(angles)
    sine = jnp.where(lane < halfway, -1.0, 1.0) * jnp.sin(angles)
    cosine = jnp.concatenate([cosine] * (rows // 8), axis=0)
    sine = jnp.concatenate([sine] * (rows // 8), axis=0)
    limits = jnp.concatenate(
        [jnp.full((1, cache_len), lengths[session], jnp.int32) for session in range(sessions)], axis=1
    )

    def rotate(vectors):
        return (vectors * cosine + pltpu.roll(vectors, halfway, 1) * sine).astype(jnp.bfloat16)

    own = received[:, TILE : TILE + EXTRA, :].astype(jnp.float32)
    pairs = devices // 2
    own = own.reshape(pairs, 2, EXTRA, width)
    own = own[:, 0] + own[:, 1]
    own_rows = kv_heads * EXTRA
    own_key = rotate(own[0:kv_heads].reshape(own_rows, width))
    own_value = own[kv_heads:].reshape(own_rows, width).astype(jnp.bfloat16)

    session = lax.broadcasted_iota(jnp.int32, (rows, sessions * cache_len), 0) % PIECE
    column = lax.broadcasted_iota(jnp.int32, (rows, sessions * cache_len), 1)
    valid = (column // cache_len == session) & (column % cache_len < limits)
    own_session = lax.broadcasted_iota(jnp.int32, (rows, own_rows), 0) % PIECE
    own_column = lax.broadcasted_iota(jnp.int32, (rows, own_rows), 1)
    contract = (((1,), (1,)), ((), ()))
    for first in range(0, kv_heads, 8):
        groups = range(first, first + 8)
        queries = [
            rotate(
                received[group * per_group : (group + 1) * per_group, 0:TILE, :]
                .reshape(rows, width)
                .astype(jnp.float32)
            )
            for group in groups
        ]
        scores = [
            jnp.where(
                valid,
                lax.dot_general(
                    query,
                    keys[:, group].reshape(sessions * cache_len, width),
                    contract,
                    preferred_element_type=jnp.float32,
                )
                * scale,
                -jnp.inf,
            )
            for query, group in zip(queries, groups)
        ]
        own_scores = [
            jnp.where(
                own_column == group * EXTRA + own_session,
                lax.dot_general(query, own_key, contract, preferred_element_type=jnp.float32) * scale,
                -jnp.inf,
            )
            for query, group in zip(queries, groups)
        ]
        highest = [
            jnp.maximum(jnp.max(cached, axis=-1, keepdims=True), jnp.max(own, axis=-1, keepdims=True))
            for cached, own in zip(scores, own_scores)
        ]
        scores = [jnp.exp(cached - high) for cached, high in zip(scores, highest)]
        own_scores = [jnp.exp(own - high) for own, high in zip(own_scores, highest)]
        shares = [
            1.0 / (jnp.sum(cached, axis=-1, keepdims=True) + jnp.sum(own, axis=-1, keepdims=True))
            for cached, own in zip(scores, own_scores)
        ]
        for cached, own, share, group in zip(scores, own_scores, shares, groups):
            attended = jnp.dot(
                (cached * share).astype(jnp.bfloat16),
                values[:, group].reshape(sessions * cache_len, width),
                preferred_element_type=jnp.float32,
            )
            attended += jnp.dot(
                (own * share).astype(jnp.bfloat16), own_value, preferred_element_type=jnp.float32
            )
            out[group * rows : (group + 1) * rows, :] = attended.astype(jnp.bfloat16)


def attend(received, keys, values, lengths):
    devices, _, width = received.shape
    whole = pl.BlockSpec(memory_space=pltpu.VMEM)
    return pl.pallas_call(
        attend_kernel,
        in_specs=[whole] * 3 + [pl.BlockSpec(memory_space=pltpu.SMEM)],
        out_shape=jax.ShapeDtypeStruct((devices * TILE, width), jnp.bfloat16),
        compiler_params=pltpu.CompilerParams(vmem_limit_bytes=8 * MIB),
        cost_estimate=pl.CostEstimate(
            flops=150_000_000, bytes_accessed=3_000_000, transcendentals=300_000
        ),
    )(received, keys, values, lengths)


def inside(array):
    return pltpu.with_memory_space_constraint(array, pltpu.VMEM)


def on_block(
    tokens, norm_gain, w_query, w_keyval, w_out, cache_keys, cache_values, session_ids, lengths, devices
):
    rows = devices * PIECE
    near, gain, near_query, near_keyval, near_keys, near_values = prefetch(
        (tokens, norm_gain, w_query, w_keyval, cache_keys, cache_values)
    )
    pack_tokens = functools.partial(norm_pack, gain=gain)
    gathered = gather_rows(tokens, near, pack_tokens, devices)
    local = project(
        query_kernel,
        gathered,
        (inside(near_query), inside(near_keyval)),
        session_ids,
        (devices, TILE + EXTRA, LANES),
        (w_query.shape[1], w_keyval.shape[0]),
    )
    received = lax.all_to_all(local, "wide", split_axis=0, concat_axis=0, tiled=True)
    attended = attend(received, inside(near_keys), inside(near_values), lengths)
    near_out, near = prefetch((w_out,), (attended,))
    gathered = gather_rows(attended, near, pack, devices)
    return project(
        out_kernel, gathered, (inside(near_out),), session_ids, (rows, w_out.shape[1]), (w_out.shape[1],)
    )


def fits_block(devices, tokens, w_query, w_keyval, cache_keys):
    sessions, kv_heads, cache_len, width = cache_keys.shape
    return (
        devices == 32
        and tokens.shape[0] == PIECE
        and sessions == PIECE
        and width == LANES
        and cache_len == LANES
        and kv_heads == KVH
        and w_query.shape[1] == 4 * LANES
        and w_keyval.shape[0] == LANES // 2
    )


def on_device(*args, devices):
    tokens, _, w_query, w_keyval, _, cache_keys = args[:6]
    if fits_block(devices, tokens, w_query, w_keyval, cache_keys):
        return on_block(*args, devices)
    return on_any(*args)


def solution(mesh):
    return jax.shard_map(
        functools.partial(on_device, devices=mesh.shape["wide"]),
        mesh=mesh,
        in_specs=(
            P(("groups", "wide"), None),
            P(),
            P(None, "wide"),
            P("wide", None),
            P(None, "wide"),
            P(("groups", "wide"), None, None, None),
            P(("groups", "wide"), None, None, None),
            P("groups"),
            P(("groups", "wide")),
        ),
        out_specs=P("groups", "wide"),
        check_vma=False,
    )
```
